256 devices in a mesh: ctx: 128 (over y, x, z), tp: 2 (over core).
Axes of the slice: x: 4, y: 4, z: 8, core: 2. Of those that a mesh axis runs over, the one named last changes fastest.
Arguments:
- queries: bfloat16 [16384, 4096], P('ctx', 'tp'), may hold values from -9 to 9
- key_rows: bfloat16 [16384, 256], P('ctx', 'tp'), may hold values from -9 to 9
- value_rows: bfloat16 [16384, 256], P('ctx', 'tp'), may hold values from -6 to 6
- hidden_in: bfloat16 [16384, 2048], P('ctx'), may hold values from -6 to 6
- out_proj: bfloat16 [4096, 2048], P('tp', 'ctx'), may hold values from -0.09375 to 0.09375
- norm_gain: bfloat16 [2048], replicated, may hold values from 0.099609375 to 1.8984375
- gate_up: bfloat16 [128, 2048, 2, 1536], P('ctx', None, None, 'tp'), may hold values from -0.125 to 0.125
- down_proj: bfloat16 [128, 1536, 2048], P('ctx', 'tp'), may hold values from -0.15625 to 0.15625
- expert_ids: int32 [16384, 8], P('ctx'), may hold values from 0 to 127, all different within a row; in each aligned block of 128 rows (0 to 127, 128 to 255, ...) at most 10 rows name the same one
- route_weight: float32 [16384, 8], P('ctx'), may hold values from 0.05 to 1
Outputs:
- layer_out: bfloat16 [16384, 2048], P('ctx', 'tp')
The draws below stay inside these ranges and needn't reach their ends.
Inputs may be any that keep to these rules, and one draw needn't show every extreme that they name: `expert_ids`: each row names 8 different experts. Within the rows of one device (128 aligned rows) no expert is named more than 10 times, a bound that some block reaches.
All inputs are finite; a program needn't handle non-finite values.
Results may differ from the reference program's by a relative error of at most 0.018.
Values may be sent and summed in bfloat16 or wider, within the bound.
No kernel may reach another device: no remote copies, remote signals or barrier semaphores. Data moves between devices by JAX's collectives and lax.ppermute only.
A program may use at most 128 MiB of HBM per device.

```python
import math
import jax
import jax.numpy as jnp
import numpy as np
from jax import lax

D = 2048
QH = 32
KVH = 2
HD = 128
FFE = 1536
TOPK = 8
TOK_DEV = 128
EXPERTS = 128
CAP = 10
TOKENS = 16384
N_CTX = 128


def draw_queries(key, part):
    key = jax.random.fold_in(key, 11)
    sampled = jnp.clip(jax.random.normal(key, (TOKENS, QH * HD), jnp.float32), -4.0, 4.0)
    return sampled.astype(jnp.bfloat16)


def draw_key_rows(key, part):
    key = jax.random.fold_in(key, 23)
    sampled = jnp.clip(jax.random.normal(key, (TOKENS, KVH * HD), jnp.float32), -4.0, 4.0)
    return sampled.astype(jnp.bfloat16)


def levels(rng, extent, cuts, low, top_value):
    gain = 1.0
    for dim, blocks in cuts:
        draws = jax.random.uniform(jax.random.fold_in(jax.random.fold_in(rng, 6), dim), (blocks,), jnp.float32, low / len(cuts), top_value / len(cuts))
        gain = gain * jnp.repeat(jnp.exp(draws), extent[dim] // blocks).reshape((-1,) + (1,) * (len(extent) - 1 - dim))
    return gain


def deal_out(rng, own, number, rows, number_of, top, reach, skew):
    sequence = jax.random.permutation(rng, number_of)
    heavy_load, ordinary = portions_of(number_of, rows * top, reach, skew, True), portions_of(number_of, rows * top, reach, skew, False)
    places = jnp.arange(number_of)

    def named(tallies, rotation):
        used = int((tallies > 0).sum())
        fixed = max(1, used // 4)
        shifted = fixed + (places - fixed + rotation * (used - fixed)) % max(1, number_of - fixed)
        return jnp.zeros((number_of,), jnp.int32).at[sequence[jnp.where(places < fixed, places, shifted)]].set(jnp.asarray(tallies, jnp.int32))

    tallies = jnp.where(number % 4 == 0, named(heavy_load, number // 4), named(ordinary, number - number // 4 - 1))
    mixed = jax.random.permutation(jax.random.fold_in(own, 3), number_of)
    giver, sink = mixed[0:number_of // 2 * 2:2], mixed[1:number_of // 2 * 2:2]
    margin = jnp.minimum(tallies[giver] - 1, reach - tallies[sink]) // 2
    margin = jnp.where((giver == sequence[0]) | (sink == sequence[0]) | (tallies[sink] == 0), 0, jnp.maximum(margin, 0))
    shifted = jax.random.randint(jax.random.fold_in(own, 4), (number_of // 2,), 0, 1 << 20) % (margin + 1)
    tallies = tallies.at[giver].add(-shifted).at[sink].add(shifted)
    labels = jnp.searchsorted(jnp.cumsum(tallies), jnp.arange(rows * top), side="right").astype(jnp.int32)
    grid = labels.reshape(top, rows).T
    grid = grid[jax.random.permutation(jax.random.fold_in(own, 1), rows)]
    rotation = jax.random.randint(jax.random.fold_in(own, 2), (rows, 1), 0, top)
    return jnp.take_along_axis(grid, (jnp.arange(top)[None, :] + rotation) % top, axis=1)


def portions_of(number_of, total, reach, slope, full):
    loads = [(1 << 20) // math.isqrt(rank ** slope) + 1 for rank in range(1, number_of + 1)]
    largest = reach if full else min(reach, max(-(-total // number_of), total * loads[0] // sum(loads)))
    least = 1 if total - largest >= number_of - 1 else 0
    given, rest = [largest] + [least] * (number_of - 1), total - largest - least * (number_of - 1)
    while rest > 0:
        candidates = [i for i in range(1, number_of) if given[i] < largest] or [i for i in range(1, number_of) if given[i] < reach]
        whole, budget = sum([loads[i] for i in candidates]), rest
        for i in candidates:
            addition = min(reach - given[i], max(1, budget * loads[i] // whole), rest)
            given[i] = given[i] + addition
            rest = rest - addition
    return np.array(given)


def normal_values(own_key, shape, scale, reach, cuts=(), kind=jnp.bfloat16):
    loudness = levels(own_key, shape, cuts, -0.22, 0.18) if cuts else 1.0
    entries = jax.random.normal(own_key, shape, jnp.float32) * scale * loudness
    return jnp.minimum(jnp.maximum(entries, -reach), reach).astype(kind)


def setup_inputs(seed: int = 0) -> dict:
    streams_of = jax.random.split(jax.random.key(seed), 11)
    queries = draw_queries(jax.random.fold_in(streams_of[10], 71), 0)
    key_rows = draw_key_rows(jax.random.fold_in(streams_of[10], 71), 0)
    value_rows = normal_values(streams_of[2], (TOKENS, KVH * HD), 1.0, 6.0, ((0, 128), (1, 2)))
    hidden_in = normal_values(streams_of[3], (TOKENS, D), 0.5, 6.0, ((0, 128),))
    out_proj = normal_values(streams_of[4], (QH * HD, D), (QH * HD) ** -0.5, 0.09375, ((0, 2), (1, 128)))
    norm_gain = jnp.clip(1.0 + 0.18 * jax.random.normal(streams_of[5], (D,), jnp.float32), 0.099609375, 1.8984375).astype(jnp.bfloat16)
    gate_up = normal_values(streams_of[6], (EXPERTS, D, 2, FFE), D ** -0.5, 0.125, ((0, 128), (3, 2)))
    down_proj = normal_values(streams_of[7], (EXPERTS, FFE, D), FFE ** -0.5, 0.15625, ((0, 128), (1, 2)))
    expert_ids_keys = jax.random.split(jax.random.fold_in(streams_of[8], 1), TOKENS // TOK_DEV)
    expert_ids_turns = jax.random.permutation(jax.random.fold_in(streams_of[8], 3), TOKENS // TOK_DEV)
    expert_ids = jax.vmap(lambda own, number: deal_out(jax.random.fold_in(streams_of[8], 2), own, number, TOK_DEV, EXPERTS, TOPK, CAP, 2))(expert_ids_keys, expert_ids_turns).reshape((TOKENS, TOPK))
    route_weight = jnp.clip(jnp.exp(math.log(1.0) - 2.9957323 * jax.random.uniform(streams_of[9], (TOKENS, TOPK), jnp.float32) ** levels(streams_of[9], (TOKENS, TOPK), ((0, 128),), -0.2, 0.2)), 0.05, 1.0)
    return {"queries": queries, "key_rows": key_rows, "value_rows": value_rows, "hidden_in": hidden_in, "out_proj": out_proj, "norm_gain": norm_gain, "gate_up": gate_up, "down_proj": down_proj, "expert_ids": expert_ids, "route_weight": route_weight}


def attend(query_blk, key_blk, value_blk, anchor_keys, anchor_values, anchor_live):
    row_count = query_blk.shape[0]
    kv_count = key_blk.shape[1] // HD
    query_view = query_blk.astype(jnp.float32).reshape(row_count, kv_count, -1, HD)
    all_keys = jnp.concatenate([anchor_keys, key_blk], axis=0).astype(jnp.float32).reshape(2 * row_count, kv_count, HD)
    all_values = jnp.concatenate([anchor_values, value_blk], axis=0).astype(jnp.float32).reshape(2 * row_count, kv_count, HD)
    scores = jnp.einsum('tkgd,skd->kgts', query_view, all_keys) * HD ** (-0.5)
    row_ids = jnp.arange(row_count, dtype=jnp.int32)
    own_ok = row_ids[None, :] <= row_ids[:, None]
    anchor_ok = jnp.broadcast_to(anchor_live, (row_count, row_count))
    visible = jnp.concatenate([anchor_ok, own_ok], axis=1)
    scores = jnp.where(visible, scores, -1e+30)
    row_peak = lax.optimization_barrier(jnp.max(scores, axis=-1, keepdims=True))
    exp_scores = jnp.exp(scores - row_peak)
    attn_probs = (exp_scores / lax.optimization_barrier(jnp.sum(exp_scores, axis=-1, keepdims=True))).astype(jnp.bfloat16)
    head_out = jnp.einsum('kgts,skd->tkgd', attn_probs.astype(jnp.float32), all_values)
    return head_out.reshape(row_count, -1).astype(jnp.bfloat16)

def reference(queries, key_rows, value_rows, hidden_in, out_proj, norm_gain, gate_up, down_proj, expert_ids, route_weight):
    query_blocks = queries.reshape(N_CTX, TOK_DEV, -1)
    key_blocks = key_rows.reshape(N_CTX, TOK_DEV, -1)
    value_blocks = value_rows.reshape(N_CTX, TOK_DEV, -1)
    anchor_keys = key_blocks[0]
    anchor_values = value_blocks[0]

    def one_block(inputs):
        query_blk, key_blk, value_blk, block_id = inputs
        return attend(query_blk, key_blk, value_blk, anchor_keys, anchor_values, block_id > 0)
    head_out = lax.map(one_block, (query_blocks, key_blocks, value_blocks, jnp.arange(N_CTX, dtype=jnp.int32)))
    head_out = head_out.reshape(TOKENS, -1)
    attn_proj = jnp.dot(head_out, out_proj, preferred_element_type=jnp.float32)
    residual = (hidden_in.astype(jnp.float32) + attn_proj).astype(jnp.bfloat16)
    resid_float = residual.astype(jnp.float32)
    mean_sq = lax.optimization_barrier(jnp.mean(resid_float * resid_float, axis=-1, keepdims=True))
    normed = (resid_float * lax.rsqrt(mean_sq + 1e-06) * norm_gain.astype(jnp.float32)).astype(jnp.bfloat16)
    flat_ids = expert_ids.reshape(N_CTX, TOK_DEV * TOPK)
    onehot = (flat_ids[:, :, None] == jnp.arange(EXPERTS, dtype=jnp.int32)[None, None, :]).astype(jnp.int32)
    earlier = jnp.cumsum(onehot, axis=1) - onehot
    slot_index = lax.optimization_barrier(jnp.sum(earlier * onehot, axis=-1))
    position = jnp.arange(N_CTX, dtype=jnp.int32)[:, None] * CAP + slot_index
    token_ids = jnp.arange(TOKENS * TOPK, dtype=jnp.int32) // TOPK
    slot_table = jnp.zeros((EXPERTS, N_CTX * CAP), jnp.int32).at[flat_ids.reshape(-1), position.reshape(-1)].set(token_ids)

    def one_expert(inputs):
        table_row, weight_gu, weight_down = inputs
        gathered = normed[table_row]
        both_parts = jnp.dot(gathered, weight_gu.reshape(D, 2 * FFE), preferred_element_type=jnp.float32)
        hidden_units = (jax.nn.silu(both_parts[:, :FFE]) * both_parts[:, FFE:]).astype(jnp.bfloat16)
        return jnp.dot(hidden_units, weight_down, preferred_element_type=jnp.float32).astype(jnp.bfloat16)
    expert_out = lax.map(one_expert, (slot_table, gate_up, down_proj))
    mix_weight = route_weight / lax.optimization_barrier(jnp.sum(route_weight, axis=-1, keepdims=True))
    pos_rows = position.reshape(TOKENS, TOPK)
    moe_sum = jnp.zeros((TOKENS, D), jnp.float32)
    for slot_rank in range(TOPK):
        picked = expert_out[expert_ids[:, slot_rank], pos_rows[:, slot_rank]].astype(jnp.float32)
        moe_sum = moe_sum + mix_weight[:, slot_rank:slot_rank + 1] * picked
    return (resid_float + moe_sum).astype(jnp.bfloat16)
```

```python
import jax
import jax.numpy as jnp
from jax import lax
from jax.sharding import Mesh, PartitionSpec as P

HD = 128
NY, NX, NZ = 4, 4, 8
PLANE = NY * NX
CAP = 10
SLOTS = NZ * CAP
F32 = jnp.float32
BF16 = jnp.bfloat16


def shift(x, axis, size, step):
    return lax.ppermute(x, axis, [(i, (i + step) % size) for i in range(size)])


def swap(x):
    return lax.ppermute(x, "tp", [(0, 1), (1, 0)])


def from_first(x):
    for axis, size in (("z", NZ), ("x", NX), ("y", NY)):
        place = lax.axis_index(axis)
        have = 1
        while have < size:
            came = lax.ppermute(x, axis, [(k, k + have) for k in range(have)])
            x = jnp.where((place >= have) & (place < 2 * have), came, x)
            have *= 2
    return x


def ring_gather_x(x):
    half = x.shape[0] // 2
    behind, ahead = shift(x, "x", NX, 1), shift(x, "x", NX, -1)
    far_a = shift(behind[:half], "x", NX, 1)
    far_b = shift(ahead[half:], "x", NX, -1)
    return [x, ahead, jnp.concatenate([far_a, far_b], axis=0), behind]


def ring_gather_z(x):
    half = x.shape[0] // 2
    right, left = [x], [x]
    for _ in range(3):
        right.append(shift(right[-1], "z", NZ, 1))
        left.append(shift(left[-1], "z", NZ, -1))
    far_a = shift(right[3][:half], "z", NZ, 1)
    far_b = shift(left[3][half:], "z", NZ, -1)
    far = jnp.concatenate([far_a, far_b], axis=0)
    return [x, left[1], left[2], left[3], far, right[3], right[2], right[1]]


def ring_scatter_z(parts):
    half = parts[0].shape[0] // 2
    far = parts[4].astype(BF16)
    go_right = shift(far[:half], "z", NZ, 1).astype(F32)
    go_left = shift(far[half:], "z", NZ, -1).astype(F32)
    go_right = jnp.concatenate([parts[3][:half] + go_right, parts[3][half:]], axis=0)
    go_left = jnp.concatenate([parts[5][:half], parts[5][half:] + go_left], axis=0)
    for r in (2, 1, 0):
        go_right = shift(go_right.astype(BF16), "z", NZ, 1).astype(F32)
        go_left = shift(go_left.astype(BF16), "z", NZ, -1).astype(F32)
        if r:
            go_right = parts[r] + go_right
            go_left = parts[NZ - r] + go_left
    return parts[0] + go_right + go_left


def attend(query_blk, key_blk, value_blk, anchor_keys, anchor_values, anchor_live):
    row_count = query_blk.shape[0]
    kv_count = key_blk.shape[1] // HD
    query_view = query_blk.reshape(row_count, kv_count, -1, HD)
    all_keys = jnp.concatenate([anchor_keys, key_blk], axis=0).reshape(2 * row_count, kv_count, HD)
    all_values = jnp.concatenate([anchor_values, value_blk], axis=0).reshape(
        2 * row_count, kv_count, HD
    )
    scores = jnp.einsum(
        "tkgd,skd->kgts", query_view, all_keys, preferred_element_type=F32
    ) * HD ** (-0.5)
    row_ids = jnp.arange(row_count, dtype=jnp.int32)
    own_ok = row_ids[None, :] <= row_ids[:, None]
    anchor_ok = jnp.broadcast_to(anchor_live, (row_count, row_count))
    visible = jnp.concatenate([anchor_ok, own_ok], axis=1)
    scores = jnp.where(visible, scores, -1e30)
    row_peak = jnp.max(scores, axis=-1, keepdims=True)
    exp_scores = jnp.exp(scores - row_peak)
    attn_probs = (exp_scores / jnp.sum(exp_scores, axis=-1, keepdims=True)).astype(BF16)
    head_out = jnp.einsum("kgts,skd->tkgd", attn_probs, all_values, preferred_element_type=F32)
    return head_out.reshape(row_count, -1).astype(BF16)


def routing(expert_ids, route_weight):
    mix = route_weight / jnp.sum(route_weight, axis=-1, keepdims=True)
    packed = jnp.concatenate([expert_ids.astype(F32), mix], axis=1)
    packed = lax.all_gather(packed, "z", axis=0, tiled=False)
    place = lax.axis_index("z")
    packed = lax.dynamic_slice_in_dim(jnp.concatenate([packed, packed], axis=0), place, NZ, 0)
    rows, top = expert_ids.shape
    ids, weights = packed[:, :, :top], packed[:, :, top:]
    mine = (jnp.arange(PLANE, dtype=jnp.int32) * NZ + place).astype(F32)
    hit = ids[:, :, None, :] == mine[None, None, :, None]
    named = jnp.any(hit, axis=-1)
    weight = jnp.sum(jnp.where(hit, weights[:, :, None, :], 0.0), axis=-1)
    earlier = jnp.tril(jnp.ones((rows, rows), BF16), -1)
    slot = jnp.einsum("ut,btp->bup", earlier, named.astype(BF16), preferred_element_type=F32)
    slot = slot + CAP * jnp.arange(NZ, dtype=F32)[:, None, None]
    slot = jnp.where(named, slot, -1.0)
    slot_t = slot.reshape(NZ * rows, PLANE).T
    weight_t = weight.reshape(NZ * rows, PLANE).T
    is_slot = slot_t[:, None, :] == jnp.arange(SLOTS, dtype=F32)[None, :, None]
    pick = is_slot.astype(BF16).reshape(PLANE * SLOTS, NZ * rows)
    combine = jnp.where(is_slot, weight_t[:, None, :], 0.0).astype(BF16)
    return pick, combine.reshape(PLANE * SLOTS, NZ * rows)


def per_device(
    queries,
    key_rows,
    value_rows,
    hidden_in,
    out_proj,
    norm_gain,
    gate_up,
    down_proj,
    expert_ids,
    route_weight,
):
    tp_rank = lax.axis_index("tp")
    x_place = lax.axis_index("x")
    block_index = lax.axis_index(("y", "x", "z"))
    rows, width = hidden_in.shape
    half = width // 2

    weight_o = lax.all_gather(out_proj.T, ("y", "z"), axis=0, tiled=True)
    anchor = from_first(jnp.concatenate([key_rows, value_rows], axis=1))
    kv_width = key_rows.shape[1]
    head_out = attend(
        queries, key_rows, value_rows, anchor[:, :kv_width], anchor[:, kv_width:], block_index > 0
    )
    group = jnp.concatenate(ring_gather_x(head_out), axis=0)
    proj = lax.dot_general(group, weight_o, (((1,), (1,)), ((), ())), preferred_element_type=F32)
    quarter = proj.shape[1] // 2
    keep = lax.dynamic_slice_in_dim(proj, tp_rank * quarter, quarter, 1)
    give = lax.dynamic_slice_in_dim(proj, (1 - tp_rank) * quarter, quarter, 1)
    summed = (keep + swap(give)).astype(BF16).reshape(NX, rows, quarter)
    pieces = [summed[0]] + [shift(summed[r], "x", NX, r) for r in (1, 2, 3)]
    by_x = jnp.stack([pieces[0], pieces[3], pieces[2], pieces[1]] * 2, axis=0)
    by_x = lax.dynamic_slice_in_dim(by_x, (NX - x_place) % NX, NX, 0)
    by_x = by_x.reshape(NX, rows, 2, quarter // 2)
    attn_proj = jnp.transpose(by_x, (1, 2, 0, 3)).reshape(rows, half).astype(F32)

    hidden_half = lax.dynamic_slice_in_dim(hidden_in, tp_rank * half, half, 1)
    resid_float = (hidden_half.astype(F32) + attn_proj).astype(BF16).astype(F32)
    sum_sq = jnp.sum(resid_float * resid_float, axis=-1, keepdims=True)
    mean_sq = (sum_sq + swap(sum_sq)) / width
    gain_half = lax.dynamic_slice_in_dim(norm_gain, tp_rank * half, half, 0)
    normed = (resid_float * lax.rsqrt(mean_sq + 1e-06) * gain_half.astype(F32)).astype(BF16)

    pick, combine = routing(expert_ids, route_weight)
    column = jnp.concatenate(ring_gather_z(normed), axis=0)
    send = jnp.dot(pick, column, preferred_element_type=F32).astype(BF16)
    send = send.reshape(PLANE, SLOTS, half)
    arrived = lax.all_to_all(send, ("y", "x"), split_axis=0, concat_axis=0, tiled=True)
    own_part = arrived.reshape(PLANE * SLOTS, half)
    other_part = swap(own_part)

    inner = gate_up.shape[3]
    gu_own = lax.dynamic_slice_in_dim(gate_up[0], tp_rank * half, half, 0).reshape(half, -1)
    gu_other = lax.dynamic_slice_in_dim(gate_up[0], (1 - tp_rank) * half, half, 0).reshape(half, -1)
    both_parts = jnp.dot(own_part, gu_own, preferred_element_type=F32) + jnp.dot(
        other_part, gu_other, preferred_element_type=F32
    )
    hidden_units = (jax.nn.silu(both_parts[:, :inner]) * both_parts[:, inner:]).astype(BF16)
    down_own = lax.dynamic_slice_in_dim(down_proj[0], tp_rank * half, half, 1)
    down_other = lax.dynamic_slice_in_dim(down_proj[0], (1 - tp_rank) * half, half, 1)
    out_other = jnp.dot(hidden_units, down_other, preferred_element_type=F32).astype(BF16)
    came = swap(out_other)
    out_own = jnp.dot(hidden_units, down_own, preferred_element_type=F32)
    expert_out = (out_own + came.astype(F32)).astype(BF16).reshape(PLANE, SLOTS, half)
    returned = lax.all_to_all(expert_out, ("y", "x"), split_axis=0, concat_axis=0, tiled=True)
    returned = returned.reshape(PLANE * SLOTS, half)
    terms = lax.dot_general(
        combine, returned, (((0,), (0,)), ((), ())), preferred_element_type=F32
    ).reshape(NZ, rows, half)
    moe_sum = ring_scatter_z([terms[r] for r in range(NZ)])
    return (resid_float + moe_sum).astype(BF16)


def solution(mesh):
    fine = Mesh(mesh.devices.reshape(NY, NX, NZ, 2), ("y", "x", "z", "tp"))
    ctx = ("y", "x", "z")
    in_specs = (
        P(ctx, "tp"),
        P(ctx, "tp"),
        P(ctx, "tp"),
        P(ctx, None),
        P("tp", ctx),
        P(),
        P(ctx, None, None, "tp"),
        P(ctx, "tp", None),
        P(ctx, None),
        P(ctx, None),
    )
    return jax.shard_map(
        per_device, mesh=fine, in_specs=in_specs, out_specs=P(ctx, "tp"), check_vma=False
    )
```

```python
import jax
import jax.numpy as jnp
from jax import lax
from jax.experimental import pallas as pl
from jax.experimental.pallas import tpu as pltpu
from jax.sharding import Mesh, PartitionSpec as P

HD = 128
NY, NX, NZ = 4, 4, 8
PLANE = NY * NX
CAP = 10
SLOTS = NZ * CAP
F32 = jnp.float32
BF16 = jnp.bfloat16
VMEM = pl.BlockSpec(memory_space=pltpu.VMEM)
SMEM = pl.BlockSpec(memory_space=pltpu.SMEM)


def shift(x, axis, size, step):
    return lax.ppermute(x, axis, [(i, (i + step) % size) for i in range(size)])


def swap(x):
    return lax.ppermute(x, "tp", [(0, 1), (1, 0)])


def call(kernel, out_shape, coords, *arrays, scratch=(), flops=0, bytes_accessed=0):
    return pl.pallas_call(
        kernel,
        out_shape=out_shape,
        in_specs=[SMEM] + [VMEM] * len(arrays),
        out_specs=jax.tree.map(lambda _: VMEM, out_shape),
        scratch_shapes=list(scratch),
        cost_estimate=pl.CostEstimate(
            flops=flops, bytes_accessed=bytes_accessed, transcendentals=0
        ),
        compiler_params=pltpu.CompilerParams(vmem_limit_bytes=40 * 1024 * 1024),
    )(coords, *arrays)


def from_first(x):
    for axis, size in (("z", NZ), ("x", NX), ("y", NY)):
        place = lax.axis_index(axis)
        have = 1
        while have < size:
            came = lax.ppermute(x, axis, [(k, k + have) for k in range(have)])
            x = jnp.where((place >= have) & (place < 2 * have), came, x)
            have *= 2
    return x


def ring4(x, axis):
    half = x.shape[0] // 2
    behind, ahead = shift(x, axis, 4, 1), shift(x, axis, 4, -1)
    return x, ahead, behind, shift(behind[:half], axis, 4, 1), shift(ahead[half:], axis, 4, -1)


def ring8(x, axis):
    half = x.shape[1] // 2
    behind, ahead = [x], [x]
    for _ in range(3):
        behind.append(shift(behind[-1], axis, 8, 1))
        ahead.append(shift(ahead[-1], axis, 8, -1))
    far = (shift(behind[3][:, :half], axis, 8, 1), shift(ahead[3][:, half:], axis, 8, -1))
    return (x, *ahead[1:], *behind[1:], *far)


def place8(out_ref, refs, rows_of):
    own, a1, a2, a3, b1, b2, b3, far_a, far_b = refs
    rows, half = own.shape[0], far_a.shape[1]
    for r, ref in ((0, own), (1, a1), (2, a2), (3, a3), (7, b1), (6, b2), (5, b3)):
        out_ref[pl.ds(rows_of(r), rows), :] = ref[...]
    out_ref[pl.ds(rows_of(4), rows), :half] = far_a[...]
    out_ref[pl.ds(rows_of(4), rows), half:] = far_b[...]


def order_kernel(coords, *refs):
    *blocks, out = refs
    z = coords[2]
    rows = blocks[0].shape[0]
    place8(out, blocks, lambda r: pl.multiple_of(lax.rem(z + r, NZ) * rows, rows))


def attend_kernel(
    coords, own, ahead, behind, far_a, far_b, anchor, w_own, w_ahead, w_behind, w_far_a, w_far_b,
    keep_ref, give_ref, qkv, head_out, weight,
):
    y, x, z, t = coords[0], coords[1], coords[2], coords[3]
    rows = own.shape[0]
    wide = own.shape[1] - 2 * HD
    half = rows // 2
    for r, ref in ((0, own), (1, ahead), (3, behind)):
        qkv[r * rows : (r + 1) * rows, :] = ref[...]
    qkv[2 * rows : 2 * rows + half, :] = far_a[...]
    qkv[2 * rows + half : 3 * rows, :] = far_b[...]

    def row_of(r):
        return pl.multiple_of(lax.rem(y + r + 4 - 2 * t, NY) * rows, rows)

    for r, ref in ((0, w_own), (1, w_ahead), (3, w_behind)):
        weight[pl.ds(row_of(r), rows), :] = ref[...]
    weight[pl.ds(row_of(2), half), :] = w_far_a[...]
    weight[pl.ds(pl.multiple_of(row_of(2) + half, half), half), :] = w_far_b[...]

    batch = 4
    shape = (batch * rows, 2 * rows)
    row_id = lax.rem(lax.broadcasted_iota(jnp.int32, shape, 0), rows)
    col_id = lax.broadcasted_iota(jnp.int32, shape, 1)
    own_ok = (col_id >= rows) & (col_id - rows <= row_id)
    for r in range(NX):
        live = (y + lax.rem(x + r, NX) + z) > 0
        visible = own_ok | ((col_id < rows) & live)
        band = slice(r * rows, (r + 1) * rows)
        keys = jnp.concatenate([anchor[:, :HD], qkv[band, wide : wide + HD]], axis=0)
        values = jnp.concatenate([anchor[:, HD:], qkv[band, wide + HD :]], axis=0)
        for first in range(0, wide // HD, batch):
            heads = range(first, first + batch)
            query = jnp.concatenate([qkv[band, h * HD : (h + 1) * HD] for h in heads], axis=0)
            scores = lax.dot_general(
                query, keys, (((1,), (1,)), ((), ())), preferred_element_type=F32
            ) * HD ** (-0.5)
            scores = jnp.where(visible, scores, -1e30)
            exp_scores = jnp.exp(scores - jnp.max(scores, axis=-1, keepdims=True))
            probs = exp_scores * (1.0 / jnp.sum(exp_scores, axis=-1, keepdims=True))
            result = jnp.dot(probs.astype(BF16), values, preferred_element_type=F32).astype(BF16)
            for i, h in enumerate(heads):
                head_out[band, h * HD : (h + 1) * HD] = result[i * rows : (i + 1) * rows]
    cut = keep_ref.shape[1]
    dims = (((1,), (1,)), ((), ()))
    give_ref[...] = lax.dot_general(
        head_out[...], weight[cut:, :], dims, preferred_element_type=F32
    )
    keep_ref[...] = lax.dot_general(
        head_out[...], weight[:cut, :], dims, preferred_element_type=F32
    )


def residual_kernel(coords, p0, p1, p2, p3, hidden, resid_ref, sq_ref):
    x, t = coords[1], coords[3]
    rows, half = resid_ref.shape
    hidden_half = hidden.at[:, pl.ds(pl.multiple_of(t * half, half), half)]
    total = jnp.zeros((rows, 1), F32)
    for r, piece in enumerate((p0, p1, p2, p3)):
        column = lax.rem(x + NX - r, NX) * HD
        for part in range(2):
            at = pl.ds(pl.multiple_of(column + part * NX * HD, HD), HD)
            term = piece[:, part * HD : (part + 1) * HD].astype(F32)
            resid = (hidden_half[:, at].astype(F32) + term).astype(BF16)
            resid_ref[:, at] = resid
            total += jnp.sum(jnp.square(resid.astype(F32)), axis=-1, keepdims=True)
    sq_ref[...] = total


def routing_kernel(coords, packed, slot_ref, weight_ref):
    z = coords[2]
    rows = packed.shape[1]
    top = packed.shape[0] // (2 * NZ)
    before = lax.broadcasted_iota(jnp.int32, (rows, rows), 0) < lax.broadcasted_iota(
        jnp.int32, (rows, rows), 1
    )
    before = before.astype(F32).astype(BF16)
    expert = lax.broadcasted_iota(jnp.int32, (PLANE, top, rows), 0) * NZ + z
    for b in range(NZ):
        ids = packed[2 * b * top : (2 * b + 1) * top, :].astype(jnp.int32)
        mix = packed[(2 * b + 1) * top : (2 * b + 2) * top, :]
        hit = ids[None] == expert
        named = jnp.sum(jnp.where(hit, 1.0, 0.0), axis=1)
        weight = jnp.sum(jnp.where(hit, mix[None], 0.0), axis=1)
        slot = jnp.dot(named.astype(BF16), before, preferred_element_type=F32) + float(b * CAP)
        slot_ref[:, b * rows : (b + 1) * rows] = jnp.where(named > 0.5, slot, -1.0)
        weight_ref[:, b * rows : (b + 1) * rows] = weight


def pick_kernel(coords, slot_ref, *refs):
    *blocks, out, column, pick = refs
    rows = blocks[0].shape[0]
    place8(column, blocks, lambda r: r * rows)
    slot_id = lax.broadcasted_iota(jnp.int32, (SLOTS, column.shape[0]), 0).astype(F32)
    for p in range(PLANE):
        hit = slot_ref[p : p + 1, :] == slot_id
        pick[p * SLOTS : (p + 1) * SLOTS, :] = jnp.where(hit, 1.0, 0.0).astype(BF16)
    for q in range(4):
        band = slice(q * 320, (q + 1) * 320)
        out[band, :] = jnp.dot(
            pick[band, :], column[...], preferred_element_type=F32
        ).astype(BF16)


def combine_kernel(coords, slot_ref, weight_ref, returned, *outs):
    *near, far_a, far_b = outs
    rows = near[0].shape[0]
    half = far_a.shape[1]
    total = PLANE * SLOTS
    column = lax.broadcasted_iota(jnp.int32, (PLANE, total), 1)
    first = lax.broadcasted_iota(jnp.int32, (PLANE, total), 0) * SLOTS
    inside = (column >= first) & (column < first + SLOTS)
    spread = jnp.where(inside, 1.0, 0.0).astype(BF16)
    slot_id = jnp.sum(jnp.where(inside, (column - first).astype(F32), 0.0), axis=0, keepdims=True)
    dims = (((0,), (0,)), ((), ()))
    for r in (4, 3, 5, 2, 6, 1, 7, 0):
        band = slice(r * rows, (r + 1) * rows)
        slot = lax.dot_general(
            slot_ref[:, band].astype(BF16), spread, dims, preferred_element_type=F32
        )
        weight = lax.dot_general(
            weight_ref[:, band].astype(BF16), spread, dims, preferred_element_type=F32
        )
        matrix = jnp.where(slot == slot_id, weight, 0.0).astype(BF16)
        term = jnp.dot(matrix, returned[...], preferred_element_type=F32)
        if r == 4:
            far_a[...] = term[:, :half].astype(BF16)
            far_b[...] = term[:, half:].astype(BF16)
        else:
            near[r if r < 4 else r - 1][...] = term


def ring_scatter_z(parts, far_a, far_b):
    half = far_a.shape[1]
    went = shift(far_a, "z", NZ, 1).astype(F32)
    came = shift(far_b, "z", NZ, -1).astype(F32)
    went = jnp.concatenate([parts[3][:, :half] + went, parts[3][:, half:]], axis=1)
    came = jnp.concatenate([parts[5][:, :half], parts[5][:, half:] + came], axis=1)
    for r in (2, 1, 0):
        went = shift(went.astype(BF16), "z", NZ, 1).astype(F32)
        came = shift(came.astype(BF16), "z", NZ, -1).astype(F32)
        if r:
            went = parts[r] + went
            came = parts[NZ - r] + came
    return parts[0] + went + came


def per_device(
    queries,
    key_rows,
    value_rows,
    hidden_in,
    out_proj,
    norm_gain,
    gate_up,
    down_proj,
    expert_ids,
    route_weight,
):
    tp_rank = lax.axis_index("tp")
    coords = jnp.stack([lax.axis_index(a) for a in ("y", "x", "z", "tp")]).astype(jnp.int32)
    rows, width = hidden_in.shape
    half = width // 2
    heads_in = out_proj.shape[0]

    anchor = from_first(jnp.concatenate([key_rows, value_rows], axis=1))
    qkv = ring4(jnp.concatenate([queries, key_rows, value_rows], axis=1), "x")
    weight_z = ring8(out_proj.T, "z")
    weight_z = call(
        order_kernel,
        jax.ShapeDtypeStruct((NZ * out_proj.shape[1], heads_in), BF16),
        coords, *weight_z, bytes_accessed=1 << 20,
    )
    weight_y = ring4(weight_z, "y")

    mix = route_weight / jnp.sum(route_weight, axis=-1, keepdims=True)
    packed = jnp.concatenate([expert_ids.T.astype(F32), mix.T], axis=0)
    for step in (1, 2, 4):
        packed = jnp.concatenate([packed, shift(packed, "z", NZ, -step)], axis=0)
    table = jax.ShapeDtypeStruct((PLANE, NZ * rows), F32)
    slot, weight = call(routing_kernel, (table, table), coords, packed, bytes_accessed=1 << 18)

    share = jax.ShapeDtypeStruct((NX * rows, width // (2 * NX)), F32)
    keep, give = call(
        attend_kernel, (share, share), coords, *qkv, anchor, *weight_y,
        scratch=[
            pltpu.VMEM((NX * rows, qkv[0].shape[1]), BF16),
            pltpu.VMEM((NX * rows, heads_in), BF16),
            pltpu.VMEM((NY * rows, heads_in), BF16),
        ],
        flops=3 * 10**9, bytes_accessed=6 << 20,
    )
    summed = (keep + swap(give)).astype(BF16).reshape(NX, rows, -1)
    pieces = [summed[0]] + [shift(summed[r], "x", NX, r) for r in (1, 2, 3)]
    resid, sum_sq = call(
        residual_kernel,
        (jax.ShapeDtypeStruct((rows, half), BF16), jax.ShapeDtypeStruct((rows, 1), F32)),
        coords, *pieces, hidden_in, bytes_accessed=1 << 20,
    )
    resid_float = resid.astype(F32)
    mean_sq = (sum_sq + swap(sum_sq)) / width
    gain_half = lax.dynamic_slice_in_dim(norm_gain, tp_rank * half, half, 0)
    normed = (resid_float * lax.rsqrt(mean_sq + 1e-06) * gain_half.astype(F32)).astype(BF16)

    column = ring8(normed, "z")
    inner = gate_up.shape[3]
    gu_own = lax.dynamic_slice_in_dim(gate_up[0], tp_rank * half, half, 0).reshape(half, -1)
    gu_other = lax.dynamic_slice_in_dim(gate_up[0], (1 - tp_rank) * half, half, 0).reshape(half, -1)
    *column, gu_own, gu_other = lax.optimization_barrier((*column, gu_own, gu_other))
    send = call(
        pick_kernel, jax.ShapeDtypeStruct((PLANE * SLOTS, half), BF16), coords, slot, *column,
        scratch=[
            pltpu.VMEM((NZ * rows, half), BF16),
            pltpu.VMEM((PLANE * SLOTS, NZ * rows), BF16),
        ],
        flops=27 * 10**8, bytes_accessed=5 << 20,
    )
    send = send.reshape(PLANE, SLOTS, half)
    arrived = lax.all_to_all(send, ("y", "x"), split_axis=0, concat_axis=0, tiled=True)
    own_part = arrived.reshape(PLANE * SLOTS, half)
    other_part = swap(own_part)

    both_parts = jnp.dot(own_part, gu_own, preferred_element_type=F32) + jnp.dot(
        other_part, gu_other, preferred_element_type=F32
    )
    hidden_units = (jax.nn.silu(both_parts[:, :inner]) * both_parts[:, inner:]).astype(BF16)
    down_own = lax.dynamic_slice_in_dim(down_proj[0], tp_rank * half, half, 1)
    down_other = lax.dynamic_slice_in_dim(down_proj[0], (1 - tp_rank) * half, half, 1)
    out_other = jnp.dot(hidden_units, down_other, preferred_element_type=F32).astype(BF16)
    came = swap(out_other)
    out_own = jnp.dot(hidden_units, down_own, preferred_element_type=F32)
    out_own, came = lax.optimization_barrier((out_own, came))
    expert_out = (out_own + came.astype(F32)).astype(BF16).reshape(PLANE, SLOTS, half)
    returned = lax.all_to_all(expert_out, ("y", "x"), split_axis=0, concat_axis=0, tiled=True)
    returned = returned.reshape(PLANE * SLOTS, half)
    near = jax.ShapeDtypeStruct((rows, half), F32)
    far = jax.ShapeDtypeStruct((rows, half // 2), BF16)
    *terms, far_a, far_b = call(
        combine_kernel, (near,) * 7 + (far,) * 2, coords, slot, weight, returned,
        flops=27 * 10**8, bytes_accessed=7 << 20,
    )
    terms = terms[:4] + [None] + terms[4:]
    moe_sum = ring_scatter_z(terms, far_a, far_b)
    return (resid_float + moe_sum).astype(BF16)


def solution(mesh):
    fine = Mesh(mesh.devices.reshape(NY, NX, NZ, 2), ("y", "x", "z", "tp"))
    ctx = ("y", "x", "z")
    in_specs = (
        P(ctx, "tp"),
        P(ctx, "tp"),
        P(ctx, "tp"),
        P(ctx, None),
        P("tp", ctx),
        P(),
        P(ctx, None, None, "tp"),
        P(ctx, "tp", None),
        P(ctx, None),
        P(ctx, None),
    )
    return jax.shard_map(
        per_device, mesh=fine, in_specs=in_specs, out_specs=P(ctx, "tp"), check_vma=False
    )
```

```python
import jax
import jax.numpy as jnp
from jax import lax
from jax.experimental import pallas as pl
from jax.experimental.pallas import tpu as pltpu
from jax.sharding import Mesh, PartitionSpec as P

HD = 128
NY, NX, NZ = 4, 4, 8
PLANE = NY * NX
CAP = 10
GROUPS = ((0, 1, 2, 7), (3, 4, 5, 6))
SLOTS = len(GROUPS[0]) * CAP
F32 = jnp.float32
BF16 = jnp.bfloat16
VMEM = pl.BlockSpec(memory_space=pltpu.VMEM)
SMEM = pl.BlockSpec(memory_space=pltpu.SMEM)
HBM = pl.BlockSpec(memory_space=pltpu.HBM)
ANY = pl.BlockSpec(memory_space=pl.ANY)


def shift(x, axis, size, step):
    return lax.ppermute(x, axis, [(i, (i + step) % size) for i in range(size)])


def swap(x):
    return lax.ppermute(x, "tp", [(0, 1), (1, 0)])


def call(
    kernel, out, coords, *arrays,
    scratch=(), flops=0, moved=0, mib=12, ins=None, outs=None, after=(),
):
    def body(coords, *refs):
        kernel(coords, *refs[len(after) :])

    return pl.pallas_call(
        body,
        out_shape=out,
        in_specs=[SMEM] + [ANY] * len(after) + (ins or [VMEM] * len(arrays)),
        out_specs=outs or jax.tree.map(lambda _: VMEM, out),
        scratch_shapes=list(scratch),
        cost_estimate=pl.CostEstimate(flops=flops, bytes_accessed=moved, transcendentals=0),
        compiler_params=pltpu.CompilerParams(vmem_limit_bytes=mib * 1024 * 1024),
    )(coords, *after, *arrays)


def shaped(shape, dtype=BF16):
    return jax.ShapeDtypeStruct(shape, dtype)


def from_first(x):
    for axis, size in (("x", NX), ("y", NY)):
        place = lax.axis_index(axis)
        have = 1
        while have < size:
            came = lax.ppermute(x, axis, [(k, k + have) for k in range(have)])
            x = jnp.where((place >= have) & (place < 2 * have), came, x)
            have *= 2
    return x


def ring8(x, axis):
    behind, ahead = [x], [x]
    for _ in range(3):
        behind.append(shift(behind[-1], axis, 8, 1))
        ahead.append(shift(ahead[-1], axis, 8, -1))
    return (*ahead, shift(behind[3], axis, 8, 1), behind[3], behind[2], behind[1])


def ring4(x, axis):
    behind, ahead = shift(x, axis, 4, 1), shift(x, axis, 4, -1)
    return x, ahead, shift(behind, axis, 4, 1), behind


def fetch(pairs, sems):
    copies = [pltpu.make_async_copy(a, b, sems.at[i]) for i, (a, b) in enumerate(pairs)]
    for copy in copies:
        copy.start()
    for copy in copies:
        copy.wait()


def join_kernel(coords, queries, keys, values, out, sems):
    wide = queries.shape[1]
    fetch(
        (
            (queries, out.at[:, :wide]),
            (keys, out.at[:, wide : wide + HD]),
            (values, out.at[:, wide + HD :]),
        ),
        sems,
    )


def pack_kernel(coords, out_proj, keys, values, ids_in, route_in, out, ids, route, sems):
    rows = out.shape[0]
    depth = out_proj.shape[1]
    pairs = [(out_proj, out.at[:, :depth]), (ids_in, ids), (route_in, route)]
    for i in range(keys.shape[0] // rows):
        band = slice(i * rows, (i + 1) * rows)
        at = depth + i * 2 * HD
        pairs.append((keys.at[band, :], out.at[:, at : at + HD]))
        pairs.append((values.at[band, :], out.at[:, at + HD : at + 2 * HD]))
    fetch(pairs, sems)
    mix = route[...] / jnp.sum(route[...], axis=0, keepdims=True)
    meta = jnp.concatenate([ids[...].astype(F32), mix], axis=0)
    out[:, out.shape[1] - HD :] = meta.astype(BF16)


def unpack_kernel(coords, *refs):
    *blocks, weight, first, meta = refs
    z = coords[2]
    rows = blocks[0].shape[0]
    depth = weight.shape[1]
    for r, ref in enumerate(blocks):
        owner = lax.rem(z + r, NZ)
        weight[pl.ds(pl.multiple_of(owner * rows, rows), rows), :] = ref[:, :depth]
        meta[r * rows : (r + 1) * rows, :] = ref[:, ref.shape[1] - HD :]

        @pl.when(owner == 0)
        def _(ref=ref):
            for i in range(first.shape[0] // rows):
                at = depth + i * 2 * HD
                first[i * rows : (i + 1) * rows, :] = ref[:, at : at + 2 * HD]


def attend_kernel(coords, own, ahead, far, behind, anchor, head_out):
    y, x, z = coords[0], coords[1], coords[2]
    rows = own.shape[0]
    wide = own.shape[1] - 2 * HD
    batch = 4
    shape = (batch * rows, 2 * rows)
    row_id = lax.rem(lax.broadcasted_iota(jnp.int32, shape, 0), rows)
    col_id = lax.broadcasted_iota(jnp.int32, shape, 1)
    own_ok = (col_id >= rows) & (col_id - rows <= row_id)
    for r, qkv in enumerate((own, ahead, far, behind)):
        live = (y + lax.rem(x + r, NX) + z) > 0
        visible = own_ok | ((col_id < rows) & live)
        band = slice(r * rows, (r + 1) * rows)
        keys = jnp.concatenate([anchor[:, :HD], qkv[:, wide : wide + HD]], axis=0)
        values = jnp.concatenate([anchor[:, HD:], qkv[:, wide + HD :]], axis=0)
        for first in range(0, wide // HD, batch):
            heads = range(first, first + batch)
            query = jnp.concatenate([qkv[:, h * HD : (h + 1) * HD] for h in heads], axis=0)
            scores = lax.dot_general(
                query, keys, (((1,), (1,)), ((), ())), preferred_element_type=F32
            ) * HD ** (-0.5)
            scores = jnp.where(visible, scores, -1e30)
            exp_scores = jnp.exp(scores - jnp.max(scores, axis=-1, keepdims=True))
            probs = exp_scores * (1.0 / jnp.sum(exp_scores, axis=-1, keepdims=True))
            result = jnp.dot(probs.astype(BF16), values, preferred_element_type=F32).astype(BF16)
            for i, h in enumerate(heads):
                head_out[band, h * HD : (h + 1) * HD] = result[i * rows : (i + 1) * rows]


def project_kernel(coords, head_out, own, ahead, far, behind, keep_ref, give_ref, weight):
    y, x, t = coords[0], coords[1], coords[3]
    rows = own.shape[0]
    for r, ref in enumerate((own, ahead, far, behind)):
        at = lax.rem(y + r + NY - 2 * t, NY) * rows
        weight[pl.ds(pl.multiple_of(at, rows), rows), :] = ref[...]
    cut = keep_ref.shape[1]
    dims = (((1,), (1,)), ((), ()))
    for ref, part in ((give_ref, slice(cut, 2 * cut)), (keep_ref, slice(0, cut))):
        result = lax.dot_general(
            head_out[...], weight[part, :], dims, preferred_element_type=F32
        )
        for r in range(NX):
            at = pl.multiple_of(lax.rem(x + r, NX) * rows, rows)
            ref[pl.ds(at, rows), :] = result[r * rows : (r + 1) * rows]


def residual_kernel(coords, attn, hidden, resid_ref, sq_ref, attn_buf, hidden_buf, sems):
    t = coords[3]
    rows, half = resid_ref.shape
    hidden_half = hidden.at[:, pl.ds(pl.multiple_of(t * half, half), half)]
    fetch(((attn, attn_buf), (hidden_half, hidden_buf)), sems)
    total = jnp.zeros((rows, 1), F32)
    for x in range(NX):
        for part in range(2):
            at = slice((part * NX + x) * HD, (part * NX + x + 1) * HD)
            term = attn_buf[x, :, part * HD : (part + 1) * HD].astype(F32)
            resid = (hidden_buf[:, at].astype(F32) + term).astype(BF16)
            resid_ref[:, at] = resid
            total += jnp.sum(jnp.square(resid.astype(F32)), axis=-1, keepdims=True)
    sq_ref[...] = total


def routing_kernel(coords, meta, *tables):
    z = coords[2]
    rows = meta.shape[1]
    top = meta.shape[0] // (2 * NZ)
    gathered = meta[...].astype(F32)
    before = lax.broadcasted_iota(jnp.int32, (rows, rows), 0) < lax.broadcasted_iota(
        jnp.int32, (rows, rows), 1
    )
    before = before.astype(F32).astype(BF16)
    expert = lax.broadcasted_iota(jnp.int32, (PLANE, top, rows), 0) * NZ + z
    for g, group in enumerate(GROUPS):
        for i, r in enumerate(group):
            table = gathered[2 * r * top : 2 * (r + 1) * top, :]
            hit = table[None, :top].astype(jnp.int32) == expert
            named = jnp.sum(jnp.where(hit, 1.0, 0.0), axis=1)
            weight = jnp.sum(jnp.where(hit, table[None, top:], 0.0), axis=1)
            slot = jnp.dot(named.astype(BF16), before, preferred_element_type=F32)
            slot = jnp.where(named > 0.5, slot + float(i * CAP), -1.0)
            tables[2 * g][:, i * rows : (i + 1) * rows] = slot
            tables[2 * g + 1][:, i * rows : (i + 1) * rows] = weight


def pick_kernel(coords, slot_ref, *refs):
    *blocks, out, column, pick, result, sem = refs
    rows = blocks[0].shape[0]
    for i, ref in enumerate(blocks):
        column[i * rows : (i + 1) * rows, :] = ref[...]
    slot_id = lax.broadcasted_iota(jnp.int32, (SLOTS, column.shape[0]), 0).astype(F32)
    for p in range(PLANE):
        hit = slot_ref[p : p + 1, :] == slot_id
        pick[p * SLOTS : (p + 1) * SLOTS, :] = jnp.where(hit, 1.0, 0.0).astype(BF16)
    for q in range(2):
        band = slice(q * 320, (q + 1) * 320)
        result[band, :] = jnp.dot(
            pick[band, :], column[...], preferred_element_type=F32
        ).astype(BF16)
    copy = pltpu.make_async_copy(result, out, sem)
    copy.start()
    copy.wait()


def expert_kernel(coords, own, other, gate_up, down, hidden, out):
    t = coords[3]
    depth = own.shape[1]
    inner = hidden.shape[1]
    mine = pl.ds(pl.multiple_of(t * depth, depth), depth)
    theirs = pl.ds(pl.multiple_of((1 - t) * depth, depth), depth)
    tile = 256
    for c in range(0, inner, tile):
        gate, up = (
            jnp.dot(own[...], gate_up[mine, at : at + tile], preferred_element_type=F32)
            + jnp.dot(other[...], gate_up[theirs, at : at + tile], preferred_element_type=F32)
            for at in (c, inner + c)
        )
        hidden[:, c : c + tile] = (gate / (1.0 + jnp.exp(-gate)) * up).astype(BF16)
    out[...] = jnp.dot(hidden[...], down[:, theirs], preferred_element_type=F32).astype(BF16)


def down_kernel(coords, hidden, down, came, out):
    depth = came.shape[1]
    mine = pl.ds(pl.multiple_of(coords[3] * depth, depth), depth)
    total = jnp.dot(hidden[...], down[:, mine], preferred_element_type=F32)
    out[...] = (total + came[...].astype(F32)).astype(BF16)


def combine_kernel(coords, slot_ref, weight_ref, returned, *outs):
    rows = outs[0].shape[0]
    total = PLANE * SLOTS
    column = lax.broadcasted_iota(jnp.int32, (PLANE, total), 1)
    first = lax.broadcasted_iota(jnp.int32, (PLANE, total), 0) * SLOTS
    inside = (column >= first) & (column < first + SLOTS)
    spread = jnp.where(inside, 1.0, 0.0).astype(BF16)
    slot_id = jnp.sum(jnp.where(inside, (column - first).astype(F32), 0.0), axis=0, keepdims=True)
    dims = (((0,), (0,)), ((), ()))
    for i, out in enumerate(outs):
        band = slice(i * rows, (i + 1) * rows)
        slot = lax.dot_general(
            slot_ref[:, band].astype(BF16), spread, dims, preferred_element_type=F32
        )
        weight = lax.dot_general(
            weight_ref[:, band].astype(BF16), spread, dims, preferred_element_type=F32
        )
        matrix = jnp.where(slot == slot_id, weight, 0.0).astype(BF16)
        term = jnp.dot(matrix, returned[...], preferred_element_type=F32)
        out[...] = term.astype(out.dtype)


def ring_scatter_z(parts):
    went, came = parts[4], parts[5]
    for r in (3, 2, 1):
        went = parts[r] + shift(went.astype(BF16), "z", NZ, 1).astype(F32)
        came = shift(came.astype(BF16), "z", NZ, -1).astype(F32)
        if r > 1:
            came = parts[NZ + 1 - r] + came
    return parts[0] + shift(went.astype(BF16), "z", NZ, 1).astype(F32) + came


def plane_exchange(rows):
    rows = rows.reshape(PLANE, SLOTS, -1)
    rows = lax.all_to_all(rows, ("y", "x"), split_axis=0, concat_axis=0, tiled=True)
    return rows.reshape(PLANE * SLOTS, -1)


def per_device(
    queries,
    key_rows,
    value_rows,
    hidden_in,
    out_proj,
    norm_gain,
    gate_up,
    down_proj,
    expert_ids,
    route_weight,
):
    tp_rank = lax.axis_index("tp")
    coords = jnp.stack([lax.axis_index(a) for a in ("y", "x", "z", "tp")]).astype(jnp.int32)
    rows, width = hidden_in.shape
    half = width // 2
    heads_in, columns = out_proj.shape
    inner = gate_up.shape[3]

    joined = call(
        join_kernel, shaped((rows, queries.shape[1] + 2 * HD)), coords,
        queries, key_rows, value_rows, moved=1 << 20, mib=60, ins=[ANY] * 3,
        scratch=[pltpu.SemaphoreType.DMA((3,))],
    )
    qkv = ring4(joined, "x")
    packed = call(
        pack_kernel, shaped((columns, 2 * heads_in + HD)), coords,
        out_proj.T, key_rows, value_rows, expert_ids.T, route_weight.T, moved=1 << 18, mib=60,
        ins=[ANY] * 5,
        scratch=[
            pltpu.VMEM(expert_ids.T.shape, jnp.int32),
            pltpu.VMEM(route_weight.T.shape, F32),
            pltpu.SemaphoreType.DMA((19,)),
        ],
    )
    weight_z, anchor, meta = call(
        unpack_kernel,
        (shaped((NZ * columns, heads_in)), shaped((rows, 2 * HD)), shaped((NZ * 16, rows))),
        coords, *ring8(packed, "z"), moved=2 << 20, mib=8,
    )
    anchor = from_first(anchor)
    weight_y = ring4(weight_z, "y")
    table = shaped((PLANE, len(GROUPS[0]) * rows), F32)
    tables = call(routing_kernel, (table,) * 4, coords, meta, moved=1 << 18, mib=4)
    head_out = call(
        attend_kernel, shaped((NX * rows, heads_in)), coords, *qkv, anchor,
        flops=2 * 10**9, moved=6 << 20,
    )
    share = shaped((NX * rows, width // (2 * NX)), F32)
    keep, give = call(
        project_kernel, (share, share), coords, head_out, *weight_y,
        scratch=[pltpu.VMEM((NY * rows, heads_in), BF16)], flops=10**9, moved=5 << 20,
    )
    summed = (keep + swap(give)).astype(BF16).reshape(NX, rows, -1)
    attn = lax.all_to_all(summed, "x", split_axis=0, concat_axis=0, tiled=True)
    resid, sum_sq = call(
        residual_kernel, (shaped((rows, half)), shaped((rows, 1), F32)), coords, attn, hidden_in,
        ins=[ANY, ANY], moved=1 << 20, mib=4,
        scratch=[
            pltpu.VMEM(attn.shape, BF16),
            pltpu.VMEM((rows, half), BF16),
            pltpu.SemaphoreType.DMA((2,)),
        ],
    )
    resid_float = resid.astype(F32)
    mean_sq = (sum_sq + swap(sum_sq)) / width
    gain_half = lax.dynamic_slice_in_dim(norm_gain, tp_rank * half, half, 0)
    normed = (resid_float * lax.rsqrt(mean_sq + 1e-06) * gain_half.astype(F32)).astype(BF16)

    gate_up = gate_up[0].reshape(width, 2 * inner)
    count = PLANE * SLOTS

    def dispatch(group, table, column):
        return call(
            pick_kernel, shaped((count, half)), coords, table, *[column[r] for r in group],
            outs=HBM, flops=7 * 10**8, moved=3 << 20,
            scratch=[
                pltpu.VMEM((len(group) * rows, half), BF16),
                pltpu.VMEM((count, len(group) * rows), BF16),
                pltpu.VMEM((count, half), BF16),
                pltpu.SemaphoreType.DMA,
            ],
        )

    def experts(own_part, other_part):
        return call(
            expert_kernel, (shaped((count, inner)), shaped((count, half))), coords,
            own_part, other_part, gate_up, down_proj[0],
            flops=5 * 10**9, moved=12 << 20, mib=14,
        )

    def finish(hidden, came, after=()):
        return call(
            down_kernel, shaped((count, half)), coords, hidden, down_proj[0], came,
            flops=10**9, moved=6 << 20, after=after,
        )

    terms = [None] * NZ

    def combine(group, slot, weight, returned):
        parts = call(
            combine_kernel,
            tuple(shaped((rows, half), BF16 if r in (4, 5) else F32) for r in group),
            coords, slot, weight, returned, flops=7 * 10**8, moved=4 << 20,
        )
        for r, part in zip(group, parts):
            terms[r] = part

    first, second = GROUPS
    column = [None] * NZ
    column[0] = normed
    column[1], column[7] = shift(normed, "z", NZ, -1), shift(normed, "z", NZ, 1)
    column[1], column[7], gate_up = lax.optimization_barrier((column[1], column[7], gate_up))
    column[2], column[6] = shift(column[1], "z", NZ, -1), shift(column[7], "z", NZ, 1)
    send_a = dispatch(first, tables[0], column)
    column[2], column[6], send_a = lax.optimization_barrier((column[2], column[6], send_a))
    column[3], column[5] = shift(column[2], "z", NZ, -1), shift(column[6], "z", NZ, 1)
    column[4] = shift(column[5], "z", NZ, 1)
    arrived_a = plane_exchange(send_a)
    send_b = dispatch(second, tables[2], column)
    send_b, arrived_a = lax.optimization_barrier((send_b, arrived_a))
    arrived_b = plane_exchange(send_b)
    hidden_a, other_a = experts(arrived_a, swap(arrived_a))
    arrived_b, hidden_a, other_a = lax.optimization_barrier((arrived_b, hidden_a, other_a))
    hidden_b, other_b = experts(arrived_b, swap(arrived_b))
    done_a = finish(hidden_a, swap(other_a))
    returned_b = plane_exchange(finish(hidden_b, swap(other_b), after=[done_a]))
    returned_a = plane_exchange(done_a)
    combine(second, tables[2], tables[3], returned_b)
    combine(first, tables[0], tables[1], returned_a)
    moe_sum = ring_scatter_z(terms)
    return (resid_float + moe_sum).astype(BF16)


def solution(mesh):
    fine = Mesh(mesh.devices.reshape(NY, NX, NZ, 2), ("y", "x", "z", "tp"))
    ctx = ("y", "x", "z")
    in_specs = (
        P(ctx, "tp"),
        P(ctx, "tp"),
        P(ctx, "tp"),
        P(ctx, None),
        P("tp", ctx),
        P(),
        P(ctx, None, None, "tp"),
        P(ctx, "tp", None),
        P(ctx, None),
        P(ctx, None),
    )
    return jax.shard_map(
        per_device, mesh=fine, in_specs=in_specs, out_specs=P(ctx, "tp"), check_vma=False
    )
```

```python
import jax
import jax.numpy as jnp
from jax import lax
from jax.experimental import pallas as pl
from jax.experimental.pallas import tpu as pltpu
from jax.sharding import Mesh, PartitionSpec as P

HD = 128
NY, NX, NZ = 4, 4, 8
PLANE = NY * NX
CAP = 10
GROUPS = ((0, 1, 2, 7), (3, 4, 5, 6))
SLOTS = len(GROUPS[0]) * CAP
F32 = jnp.float32
BF16 = jnp.bfloat16
VMEM = pl.BlockSpec(memory_space=pltpu.VMEM)
SMEM = pl.BlockSpec(memory_space=pltpu.SMEM)
HBM = pl.BlockSpec(memory_space=pltpu.HBM)
ANY = pl.BlockSpec(memory_space=pl.ANY)


def shift(x, axis, size, step):
    return lax.ppermute(x, axis, [(i, (i + step) % size) for i in range(size)])


def swap(x):
    return lax.ppermute(x, "tp", [(0, 1), (1, 0)])


def call(
    kernel, out, coords, *arrays,
    scratch=(), flops=0, moved=0, mib=12, ins=None, outs=None, after=(),
):
    def body(coords, *refs):
        kernel(coords, *refs[len(after) :])

    return pl.pallas_call(
        body,
        out_shape=out,
        in_specs=[SMEM] + [ANY] * len(after) + (ins or [VMEM] * len(arrays)),
        out_specs=outs or jax.tree.map(lambda _: VMEM, out),
        scratch_shapes=list(scratch),
        cost_estimate=pl.CostEstimate(flops=flops, bytes_accessed=moved, transcendentals=0),
        compiler_params=pltpu.CompilerParams(vmem_limit_bytes=mib * 1024 * 1024),
    )(coords, *after, *arrays)


def shaped(shape, dtype=BF16):
    return jax.ShapeDtypeStruct(shape, dtype)


def from_first(x):
    for axis, size in (("x", NX), ("y", NY)):
        place = lax.axis_index(axis)
        have = 1
        while have < size:
            came = lax.ppermute(x, axis, [(k, k + have) for k in range(have)])
            x = jnp.where((place >= have) & (place < 2 * have), came, x)
            have *= 2
    return x


def ring8(x, axis):
    behind, ahead = [x], [x]
    for _ in range(3):
        behind.append(shift(behind[-1], axis, 8, 1))
        ahead.append(shift(ahead[-1], axis, 8, -1))
    return (*ahead, shift(behind[3], axis, 8, 1), behind[3], behind[2], behind[1])


def ring4(x, axis):
    behind, ahead = shift(x, axis, 4, 1), shift(x, axis, 4, -1)
    return x, ahead, shift(ahead, axis, 4, -1), behind


def fetch(pairs, sems):
    copies = [pltpu.make_async_copy(a, b, sems.at[i]) for i, (a, b) in enumerate(pairs)]
    for copy in copies:
        copy.start()
    for copy in copies:
        copy.wait()


def pack_kernel(
    coords, out_proj, queries, keys, values, ids_in, route_in, joined, out, ids, route, sems
):
    rows = out.shape[0]
    depth, wide = out_proj.shape[1], queries.shape[1]
    pairs = [
        (out_proj, out.at[:, :depth]),
        (ids_in, ids),
        (route_in, route),
        (queries, joined.at[:, :wide]),
        (keys, joined.at[:, wide : wide + HD]),
        (values, joined.at[:, wide + HD :]),
    ]
    for i in range(keys.shape[0] // rows):
        band = slice(i * rows, (i + 1) * rows)
        at = depth + i * 2 * HD
        pairs.append((keys.at[band, :], out.at[:, at : at + HD]))
        pairs.append((values.at[band, :], out.at[:, at + HD : at + 2 * HD]))
    fetch(pairs, sems)
    mix = route[...] / jnp.sum(route[...], axis=0, keepdims=True)
    meta = jnp.concatenate([ids[...].astype(F32), mix], axis=0)
    out[:, out.shape[1] - HD :] = meta.astype(BF16)


def unpack_kernel(coords, *refs):
    *blocks, weight, first, meta = refs
    z = coords[2]
    rows = blocks[0].shape[0]
    depth = weight.shape[1]
    for r, ref in enumerate(blocks):
        owner = lax.rem(z + r, NZ)
        weight[pl.ds(pl.multiple_of(owner * rows, rows), rows), :] = ref[:, :depth]
        meta[r * rows : (r + 1) * rows, :] = ref[:, ref.shape[1] - HD :]

        @pl.when(owner == 0)
        def _(ref=ref):
            for i in range(first.shape[0] // rows):
                at = depth + i * 2 * HD
                first[i * rows : (i + 1) * rows, :] = ref[:, at : at + 2 * HD]


def attend_kernel(coords, own, ahead, far, behind, anchor, head_out):
    y, x, z = coords[0], coords[1], coords[2]
    rows = own.shape[0]
    wide = own.shape[1] - 2 * HD
    batch = 4
    shape = (batch * rows, 2 * rows)
    row_id = lax.rem(lax.broadcasted_iota(jnp.int32, shape, 0), rows)
    col_id = lax.broadcasted_iota(jnp.int32, shape, 1)
    own_ok = (col_id >= rows) & (col_id - rows <= row_id)
    for r, qkv in enumerate((own, ahead, far, behind)):
        live = (y + lax.rem(x + r, NX) + z) > 0
        visible = own_ok | ((col_id < rows) & live)
        band = slice(r * rows, (r + 1) * rows)
        keys = jnp.concatenate([anchor[:, :HD], qkv[:, wide : wide + HD]], axis=0)
        values = jnp.concatenate([anchor[:, HD:], qkv[:, wide + HD :]], axis=0)
        for first in range(0, wide // HD, batch):
            heads = range(first, first + batch)
            query = jnp.concatenate([qkv[:, h * HD : (h + 1) * HD] for h in heads], axis=0)
            scores = lax.dot_general(
                query, keys, (((1,), (1,)), ((), ())), preferred_element_type=F32
            ) * HD ** (-0.5)
            scores = jnp.where(visible, scores, -1e30)
            exp_scores = jnp.exp(scores - jnp.max(scores, axis=-1, keepdims=True))
            probs = exp_scores * (1.0 / jnp.sum(exp_scores, axis=-1, keepdims=True))
            result = jnp.dot(probs.astype(BF16), values, preferred_element_type=F32).astype(BF16)
            for i, h in enumerate(heads):
                head_out[band, h * HD : (h + 1) * HD] = result[i * rows : (i + 1) * rows]


def project_kernel(coords, head_out, own, ahead, far, behind, keep_ref, give_ref, weight):
    y, x, t = coords[0], coords[1], coords[3]
    rows = own.shape[0]
    for r, ref in enumerate((own, ahead, far, behind)):
        at = lax.rem(y + r + NY - 2 * t, NY) * rows
        weight[pl.ds(pl.multiple_of(at, rows), rows), :] = ref[...]
    cut = keep_ref.shape[1]
    dims = (((1,), (1,)), ((), ()))
    for ref, part in ((give_ref, slice(cut, 2 * cut)), (keep_ref, slice(0, cut))):
        result = lax.dot_general(
            head_out[...], weight[part, :], dims, preferred_element_type=F32
        )
        for r in range(NX):
            at = pl.multiple_of(lax.rem(x + r, NX) * rows, rows)
            ref[pl.ds(at, rows), :] = result[r * rows : (r + 1) * rows].astype(ref.dtype)


def residual_kernel(coords, attn, hidden, resid_ref, sq_ref, attn_buf, hidden_buf, sems):
    t = coords[3]
    rows, half = resid_ref.shape
    hidden_half = hidden.at[:, pl.ds(pl.multiple_of(t * half, half), half)]
    fetch(((attn, attn_buf), (hidden_half, hidden_buf)), sems)
    total = jnp.zeros((rows, 1), F32)
    for x in range(NX):
        for part in range(2):
            at = slice((part * NX + x) * HD, (part * NX + x + 1) * HD)
            term = attn_buf[x, :, part * HD : (part + 1) * HD].astype(F32)
            resid = (hidden_buf[:, at].astype(F32) + term).astype(BF16)
            resid_ref[:, at] = resid
            total += jnp.sum(jnp.square(resid.astype(F32)), axis=-1, keepdims=True)
    sq_ref[...] = total


def routing_kernel(coords, meta, *tables):
    z = coords[2]
    rows = meta.shape[1]
    top = meta.shape[0] // (2 * NZ)
    gathered = meta[...].astype(F32)
    before = lax.broadcasted_iota(jnp.int32, (rows, rows), 0) < lax.broadcasted_iota(
        jnp.int32, (rows, rows), 1
    )
    before = before.astype(F32).astype(BF16)
    expert = lax.broadcasted_iota(jnp.int32, (PLANE, top, rows), 0) * NZ + z
    for g, group in enumerate(GROUPS):
        for i, r in enumerate(group):
            table = gathered[2 * r * top : 2 * (r + 1) * top, :]
            hit = table[None, :top].astype(jnp.int32) == expert
            named = jnp.sum(jnp.where(hit, 1.0, 0.0), axis=1)
            weight = jnp.sum(jnp.where(hit, table[None, top:], 0.0), axis=1)
            slot = jnp.dot(named.astype(BF16), before, preferred_element_type=F32)
            slot = jnp.where(named > 0.5, slot + float(i * CAP), -1.0)
            tables[2 * g][:, i * rows : (i + 1) * rows] = slot
            tables[2 * g + 1][:, i * rows : (i + 1) * rows] = weight


def pick_kernel(coords, slot_ref, *refs):
    *blocks, out, column, pick, result, sem = refs
    rows = blocks[0].shape[0]
    for i, ref in enumerate(blocks):
        column[i * rows : (i + 1) * rows, :] = ref[...]
    slot_id = lax.broadcasted_iota(jnp.int32, (SLOTS, column.shape[0]), 0).astype(F32)
    for p in range(PLANE):
        hit = slot_ref[p : p + 1, :] == slot_id
        pick[p * SLOTS : (p + 1) * SLOTS, :] = jnp.where(hit, 1.0, 0.0).astype(BF16)
    for q in range(2):
        band = slice(q * 320, (q + 1) * 320)
        result[band, :] = jnp.dot(
            pick[band, :], column[...], preferred_element_type=F32
        ).astype(BF16)
    copy = pltpu.make_async_copy(result, out, sem)
    copy.start()
    copy.wait()


def expert_kernel(coords, own, other, gate_up, down, hidden, out):
    t = coords[3]
    depth = own.shape[1]
    inner = hidden.shape[1]
    mine = pl.ds(pl.multiple_of(t * depth, depth), depth)
    theirs = pl.ds(pl.multiple_of((1 - t) * depth, depth), depth)
    tile = 256
    for c in range(0, inner, tile):
        gate, up = (
            jnp.dot(own[...], gate_up[mine, at : at + tile], preferred_element_type=F32)
            + jnp.dot(other[...], gate_up[theirs, at : at + tile], preferred_element_type=F32)
            for at in (c, inner + c)
        )
        hidden[:, c : c + tile] = (gate / (1.0 + jnp.exp(-gate)) * up).astype(BF16)
    out[...] = jnp.dot(hidden[...], down[:, theirs], preferred_element_type=F32).astype(BF16)


def down_kernel(coords, hidden, down, came, out):
    depth = came.shape[1]
    mine = pl.ds(pl.multiple_of(coords[3] * depth, depth), depth)
    total = jnp.dot(hidden[...], down[:, mine], preferred_element_type=F32)
    out[...] = (total + came[...].astype(F32)).astype(BF16)


def combine_kernel(coords, slot_ref, weight_ref, returned, *outs):
    rows = outs[0].shape[0]
    total = PLANE * SLOTS
    column = lax.broadcasted_iota(jnp.int32, (PLANE, total), 1)
    first = lax.broadcasted_iota(jnp.int32, (PLANE, total), 0) * SLOTS
    inside = (column >= first) & (column < first + SLOTS)
    spread = jnp.where(inside, 1.0, 0.0).astype(BF16)
    slot_id = jnp.sum(jnp.where(inside, (column - first).astype(F32), 0.0), axis=0, keepdims=True)
    dims = (((0,), (0,)), ((), ()))
    for i, out in enumerate(outs):
        band = slice(i * rows, (i + 1) * rows)
        slot = lax.dot_general(
            slot_ref[:, band].astype(BF16), spread, dims, preferred_element_type=F32
        )
        weight = lax.dot_general(
            weight_ref[:, band].astype(BF16), spread, dims, preferred_element_type=F32
        )
        matrix = jnp.where(slot == slot_id, weight, 0.0).astype(BF16)
        term = jnp.dot(matrix, returned[...], preferred_element_type=F32)
        out[...] = term.astype(out.dtype)


def plane_exchange(rows):
    rows = rows.reshape(PLANE, SLOTS, -1)
    rows = lax.all_to_all(rows, ("y", "x"), split_axis=0, concat_axis=0, tiled=True)
    return rows.reshape(PLANE * SLOTS, -1)


def per_device(
    queries,
    key_rows,
    value_rows,
    hidden_in,
    out_proj,
    norm_gain,
    gate_up,
    down_proj,
    expert_ids,
    route_weight,
):
    tp_rank = lax.axis_index("tp")
    coords = jnp.stack([lax.axis_index(a) for a in ("y", "x", "z", "tp")]).astype(jnp.int32)
    rows, width = hidden_in.shape
    half = width // 2
    heads_in, columns = out_proj.shape
    inner = gate_up.shape[3]

    joined, packed = call(
        pack_kernel,
        (shaped((rows, queries.shape[1] + 2 * HD)), shaped((columns, 2 * heads_in + HD))), coords,
        out_proj.T, queries, key_rows, value_rows, expert_ids.T, route_weight.T,
        moved=1 << 20, mib=60, ins=[ANY] * 6,
        scratch=[
            pltpu.VMEM(expert_ids.T.shape, jnp.int32),
            pltpu.VMEM(route_weight.T.shape, F32),
            pltpu.SemaphoreType.DMA((22,)),
        ],
    )
    qkv = ring4(joined, "x")
    weight_z, anchor, meta = call(
        unpack_kernel,
        (shaped((NZ * columns, heads_in)), shaped((rows, 2 * HD)), shaped((NZ * 16, rows))),
        coords, *ring8(packed, "z"), moved=2 << 20, mib=8,
    )
    anchor = from_first(anchor)
    weight_y = ring4(weight_z, "y")
    table = shaped((PLANE, len(GROUPS[0]) * rows), F32)
    tables = call(routing_kernel, (table,) * 4, coords, meta, moved=1 << 18, mib=4)
    head_out = call(
        attend_kernel, shaped((NX * rows, heads_in)), coords, *qkv, anchor,
        flops=2 * 10**9, moved=6 << 20,
    )
    share = (NX * rows, width // (2 * NX))
    keep, give = call(
        project_kernel, (shaped(share, F32), shaped(share)), coords, head_out, *weight_y,
        scratch=[pltpu.VMEM((NY * rows, heads_in), BF16)], flops=10**9, moved=5 << 20,
    )
    summed = (keep + swap(give)).astype(BF16).reshape(NX, rows, -1)
    attn = lax.all_to_all(summed, "x", split_axis=0, concat_axis=0, tiled=True)
    resid, sum_sq = call(
        residual_kernel, (shaped((rows, half)), shaped((rows, 1), F32)), coords, attn, hidden_in,
        ins=[ANY, ANY], moved=1 << 20, mib=4,
        scratch=[
            pltpu.VMEM(attn.shape, BF16),
            pltpu.VMEM((rows, half), BF16),
            pltpu.SemaphoreType.DMA((2,)),
        ],
    )
    resid_float = resid.astype(F32)
    mean_sq = (sum_sq + swap(sum_sq)) / width
    gain_half = lax.dynamic_slice_in_dim(norm_gain, tp_rank * half, half, 0)
    normed = (resid_float * lax.rsqrt(mean_sq + 1e-06) * gain_half.astype(F32)).astype(BF16)

    gate_up = gate_up[0].reshape(width, 2 * inner)
    count = PLANE * SLOTS

    def dispatch(group, table, column, after=()):
        return call(
            pick_kernel, shaped((count, half)), coords, table, *[column[r] for r in group],
            outs=HBM, flops=7 * 10**8, moved=3 << 20, after=after,
            scratch=[
                pltpu.VMEM((len(group) * rows, half), BF16),
                pltpu.VMEM((count, len(group) * rows), BF16),
                pltpu.VMEM((count, half), BF16),
                pltpu.SemaphoreType.DMA,
            ],
        )

    def experts(own_part, other_part, after=()):
        return call(
            expert_kernel, (shaped((count, inner)), shaped((count, half))), coords,
            own_part, other_part, gate_up, down_proj[0],
            flops=5 * 10**9, moved=12 << 20, mib=14, after=after,
        )

    def finish(hidden, came, after=()):
        return call(
            down_kernel, shaped((count, half)), coords, hidden, down_proj[0], came,
            flops=10**9, moved=6 << 20, after=after,
        )

    terms = [None] * NZ

    def combine(group, slot, weight, returned, after=()):
        parts = call(
            combine_kernel,
            tuple(shaped((rows, half), BF16 if r in (4, 5) else F32) for r in group),
            coords, slot, weight, returned, after=after,
        )
        for r, part in zip(group, parts):
            terms[r] = part

    first, second = GROUPS
    column = [None] * NZ
    column[0] = normed
    column[1], column[7] = shift(normed, "z", NZ, -1), shift(normed, "z", NZ, 1)
    column[2], column[6] = shift(column[1], "z", NZ, -1), shift(column[7], "z", NZ, 1)
    send_a = dispatch(first, tables[0], column, after=[gate_up])
    column[2], column[6], send_a = lax.optimization_barrier((column[2], column[6], send_a))
    column[3], column[5] = shift(column[2], "z", NZ, -1), shift(column[6], "z", NZ, 1)
    column[4] = shift(column[5], "z", NZ, 1)
    arrived_a = plane_exchange(send_a)
    send_b = dispatch(second, tables[2], column)
    send_b, arrived_a = lax.optimization_barrier((send_b, arrived_a))
    arrived_b = plane_exchange(send_b)
    hidden_a, other_a = experts(arrived_a, swap(arrived_a), after=[arrived_b])
    hidden_b, other_b = experts(arrived_b, swap(arrived_b), after=[hidden_a])
    done_a = finish(hidden_a, swap(other_a))
    returned_b = plane_exchange(finish(hidden_b, swap(other_b), after=[done_a]))
    returned_a = plane_exchange(done_a)
    combine(second, tables[2], tables[3], returned_b)
    went = terms[3] + shift(terms[4], "z", NZ, 1).astype(F32)
    came = terms[6] + shift(terms[5], "z", NZ, -1).astype(F32)
    went, came = shift(went.astype(BF16), "z", NZ, 1), shift(came.astype(BF16), "z", NZ, -1)
    combine(first, tables[0], tables[1], returned_a, after=[went, came])
    went = shift((terms[2] + went.astype(F32)).astype(BF16), "z", NZ, 1)
    came = shift((terms[7] + came.astype(F32)).astype(BF16), "z", NZ, -1)
    went = shift((terms[1] + went.astype(F32)).astype(BF16), "z", NZ, 1)
    moe_sum = terms[0] + went.astype(F32) + came.astype(F32)
    return (resid_float + moe_sum).astype(BF16)


def solution(mesh):
    fine = Mesh(mesh.devices.reshape(NY, NX, NZ, 2), ("y", "x", "z", "tp"))
    ctx = ("y", "x", "z")
    in_specs = (
        P(ctx, "tp"),
        P(ctx, "tp"),
        P(ctx, "tp"),
        P(ctx, None),
        P("tp", ctx),
        P(),
        P(ctx, None, None, "tp"),
        P(ctx, "tp", None),
        P(ctx, None),
        P(ctx, None),
    )
    return jax.shard_map(
        per_device, mesh=fine, in_specs=in_specs, out_specs=P(ctx, "tp"), check_vma=False
    )
```

```python
import functools

import jax
import jax.numpy as jnp
from jax import lax
from jax.experimental import pallas as pl
from jax.experimental.pallas import tpu as pltpu
from jax.sharding import Mesh, PartitionSpec as P

HD = 128
NY, NX, NZ = 4, 4, 8
PLANE = NY * NX
CAP = 10
GROUPS = ((0, 1, 2, 7), (3, 4, 5, 6))
SLOTS = len(GROUPS[0]) * CAP
F32 = jnp.float32
BF16 = jnp.bfloat16
VMEM = pl.BlockSpec(memory_space=pltpu.VMEM)
SMEM = pl.BlockSpec(memory_space=pltpu.SMEM)
HBM = pl.BlockSpec(memory_space=pltpu.HBM)
ANY = pl.BlockSpec(memory_space=pl.ANY)


def shift(x, axis, size, step):
    return lax.ppermute(x, axis, [(i, (i + step) % size) for i in range(size)])


def swap(x):
    return lax.ppermute(x, "tp", [(0, 1), (1, 0)])


def call(
    kernel, out, coords, *arrays,
    scratch=(), flops=0, moved=0, mib=12, ins=None, outs=None, after=(),
):
    def body(coords, *refs):
        kernel(coords, *refs[len(after) :])

    return pl.pallas_call(
        body,
        out_shape=out,
        in_specs=[SMEM] + [ANY] * len(after) + (ins or [VMEM] * len(arrays)),
        out_specs=outs or jax.tree.map(lambda _: VMEM, out),
        scratch_shapes=list(scratch),
        cost_estimate=pl.CostEstimate(flops=flops, bytes_accessed=moved, transcendentals=0),
        compiler_params=pltpu.CompilerParams(vmem_limit_bytes=mib * 1024 * 1024),
    )(coords, *after, *arrays)


def shaped(shape, dtype=BF16):
    return jax.ShapeDtypeStruct(shape, dtype)


def from_first(x):
    for axis, size in (("x", NX), ("y", NY)):
        place = lax.axis_index(axis)
        have = 1
        while have < size:
            came = lax.ppermute(x, axis, [(k, k + have) for k in range(have)])
            x = jnp.where((place >= have) & (place < 2 * have), came, x)
            have *= 2
    return x


def ring8(x, axis):
    behind, ahead = [x], [x]
    for _ in range(3):
        behind.append(shift(behind[-1], axis, 8, 1))
        ahead.append(shift(ahead[-1], axis, 8, -1))
    return (*ahead, shift(behind[3], axis, 8, 1), behind[3], behind[2], behind[1])


def ring4(x, axis):
    behind, ahead = shift(x, axis, 4, 1), shift(x, axis, 4, -1)
    return x, ahead, shift(ahead, axis, 4, -1), behind


def fetch(pairs, sems):
    copies = [pltpu.make_async_copy(a, b, sems.at[i]) for i, (a, b) in enumerate(pairs)]
    for copy in copies:
        copy.start()
    for copy in copies:
        copy.wait()


def pack_kernel(
    coords, out_proj, queries, keys, values, ids_in, route_in, joined, out, ids, route, sems
):
    rows = out.shape[0]
    depth, wide = out_proj.shape[1], queries.shape[1]
    fetch(
        (
            (keys, joined.at[:, wide : wide + HD]),
            (values, joined.at[:, wide + HD :]),
            (out_proj, out.at[:, :depth]),
            (ids_in, ids),
            (route_in, route),
            (queries, joined.at[:, :wide]),
        ),
        sems,
    )
    for i in range(keys.shape[0] // rows):
        at = depth + i * 2 * HD
        out[:, at : at + 2 * HD] = joined[i * rows : (i + 1) * rows, wide:]
    mix = route[...] / jnp.sum(route[...], axis=0, keepdims=True)
    meta = jnp.concatenate([ids[...].astype(F32), mix], axis=0)
    out[:, out.shape[1] - HD :] = meta.astype(BF16)


def unpack_kernel(coords, *refs):
    *blocks, weight, first, meta = refs
    z = coords[2]
    rows = blocks[0].shape[0]
    depth = weight.shape[1]
    for r, ref in enumerate(blocks):
        owner = lax.rem(z + r, NZ)
        weight[pl.ds(pl.multiple_of(owner * rows, rows), rows), :] = ref[:, :depth]
        meta[r * rows : (r + 1) * rows, :] = ref[:, ref.shape[1] - HD :]

        @pl.when(owner == 0)
        def _(ref=ref):
            for i in range(first.shape[0] // rows):
                at = depth + i * 2 * HD
                first[i * rows : (i + 1) * rows, :] = ref[:, at : at + 2 * HD]


def attend_kernel(coords, own, ahead, far, behind, anchor, head_out):
    y, x, z = coords[0], coords[1], coords[2]
    rows = own.shape[0]
    wide = own.shape[1] - 2 * HD
    batch = 4
    shape = (batch * rows, 2 * rows)
    row_id = lax.rem(lax.broadcasted_iota(jnp.int32, shape, 0), rows)
    col_id = lax.broadcasted_iota(jnp.int32, shape, 1)
    own_ok = (col_id >= rows) & (col_id - rows <= row_id)
    for r, qkv in enumerate((own, ahead, far, behind)):
        live = (y + lax.rem(x + r, NX) + z) > 0
        visible = own_ok | ((col_id < rows) & live)
        band = slice(r * rows, (r + 1) * rows)
        keys = jnp.concatenate([anchor[:, :HD], qkv[:, wide : wide + HD]], axis=0)
        values = jnp.concatenate([anchor[:, HD:], qkv[:, wide + HD :]], axis=0)
        for first in range(0, wide // HD, batch):
            heads = range(first, first + batch)
            query = jnp.concatenate([qkv[:, h * HD : (h + 1) * HD] for h in heads], axis=0)
            scores = lax.dot_general(
                query, keys, (((1,), (1,)), ((), ())), preferred_element_type=F32
            ) * HD ** (-0.5)
            scores = jnp.where(visible, scores, -1e30)
            exp_scores = jnp.exp(scores - jnp.max(scores, axis=-1, keepdims=True))
            probs = exp_scores * (1.0 / jnp.sum(exp_scores, axis=-1, keepdims=True))
            result = jnp.dot(probs.astype(BF16), values, preferred_element_type=F32).astype(BF16)
            for i, h in enumerate(heads):
                head_out[band, h * HD : (h + 1) * HD] = result[i * rows : (i + 1) * rows]


def project_kernel(coords, head_out, own, ahead, far, behind, keep_ref, give_ref, weight):
    y, t = coords[0], coords[3]
    rows = own.shape[0]
    for r, ref in enumerate((own, ahead, far, behind)):
        at = lax.rem(y + r + NY - 2 * t, NY) * rows
        weight[pl.ds(pl.multiple_of(at, rows), rows), :] = ref[...]
    cut = keep_ref.shape[1]
    dims = (((1,), (1,)), ((), ()))
    for ref, part in ((give_ref, slice(cut, 2 * cut)), (keep_ref, slice(0, cut))):
        result = lax.dot_general(
            head_out[...], weight[part, :], dims, preferred_element_type=F32
        )
        ref[...] = result.astype(ref.dtype)


def residual_kernel(
    coords, p0, p1, p2, p3, hidden, resid_ref, sq_ref, pieces, hidden_buf, sems
):
    x, t = coords[1], coords[3]
    rows, half = resid_ref.shape
    hidden_half = hidden.at[:, pl.ds(pl.multiple_of(t * half, half), half)]
    fetch(
        [(p, pieces.at[r]) for r, p in enumerate((p0, p1, p2, p3))] + [(hidden_half, hidden_buf)],
        sems,
    )
    total = jnp.zeros((rows, 1), F32)
    for r in range(NX):
        for part in range(2):
            at = (part * NX + lax.rem(x + NX - r, NX)) * HD
            at = pl.ds(pl.multiple_of(at, HD), HD)
            term = pieces[r, :, part * HD : (part + 1) * HD].astype(F32)
            resid = (hidden_buf[:, at].astype(F32) + term).astype(BF16)
            resid_ref[:, at] = resid
            total += jnp.sum(jnp.square(resid.astype(F32)), axis=-1, keepdims=True)
    sq_ref[...] = total


def routing_kernel(coords, meta, *tables):
    z = coords[2]
    rows = meta.shape[1]
    top = meta.shape[0] // (2 * NZ)
    gathered = meta[...].astype(F32)
    before = lax.broadcasted_iota(jnp.int32, (rows, rows), 0) < lax.broadcasted_iota(
        jnp.int32, (rows, rows), 1
    )
    before = before.astype(F32).astype(BF16)
    expert = lax.broadcasted_iota(jnp.int32, (PLANE, top, rows), 0) * NZ + z
    for g, group in enumerate(GROUPS):
        for i, r in enumerate(group):
            table = gathered[2 * r * top : 2 * (r + 1) * top, :]
            hit = table[None, :top].astype(jnp.int32) == expert
            named = jnp.sum(jnp.where(hit, 1.0, 0.0), axis=1)
            weight = jnp.sum(jnp.where(hit, table[None, top:], 0.0), axis=1)
            slot = jnp.dot(named.astype(BF16), before, preferred_element_type=F32)
            slot = jnp.where(named > 0.5, slot + float(i * CAP), -1.0)
            tables[2 * g][:, i * rows : (i + 1) * rows] = slot
            tables[2 * g + 1][:, i * rows : (i + 1) * rows] = weight


def pick_kernel(coords, slot_ref, *refs):
    *blocks, out, column, pick, result, sems = refs
    rows = blocks[0].shape[0]
    fetch([(b, column.at[i * rows : (i + 1) * rows, :]) for i, b in enumerate(blocks)], sems)
    slot_id = lax.broadcasted_iota(jnp.int32, (SLOTS, column.shape[0]), 0).astype(F32)
    for p in range(PLANE):
        hit = slot_ref[p : p + 1, :] == slot_id
        pick[p * SLOTS : (p + 1) * SLOTS, :] = jnp.where(hit, 1.0, 0.0).astype(BF16)
    for q in range(2):
        band = slice(q * 320, (q + 1) * 320)
        result[band, :] = jnp.dot(
            pick[band, :], column[...], preferred_element_type=F32
        ).astype(BF16)
    fetch([(result, out)], sems)


def expert_kernel(coords, own, other, gate_up, down, hidden, out):
    t = coords[3]
    depth = own.shape[1]
    inner = hidden.shape[1]
    mine = pl.ds(pl.multiple_of(t * depth, depth), depth)
    theirs = pl.ds(pl.multiple_of((1 - t) * depth, depth), depth)
    tile = 256
    for c in range(0, inner, tile):
        gate, up = (
            jnp.dot(own[...], gate_up[mine, at : at + tile], preferred_element_type=F32)
            + jnp.dot(other[...], gate_up[theirs, at : at + tile], preferred_element_type=F32)
            for at in (c, inner + c)
        )
        hidden[:, c : c + tile] = (gate / (1.0 + jnp.exp(-gate)) * up).astype(BF16)
    out[...] = jnp.dot(hidden[...], down[:, theirs], preferred_element_type=F32).astype(BF16)


def down_kernel(coords, hidden, down, came, out):
    depth = came.shape[1]
    mine = pl.ds(pl.multiple_of(coords[3] * depth, depth), depth)
    total = jnp.dot(hidden[...], down[:, mine], preferred_element_type=F32)
    out[...] = (total + came[...].astype(F32)).astype(BF16)


def combine_kernel(places, coords, slot_ref, weight_ref, returned, *outs):
    rows = outs[0].shape[0]
    total = PLANE * SLOTS
    column = lax.broadcasted_iota(jnp.int32, (PLANE, total), 1)
    first = lax.broadcasted_iota(jnp.int32, (PLANE, total), 0) * SLOTS
    inside = (column >= first) & (column < first + SLOTS)
    spread = jnp.where(inside, 1.0, 0.0).astype(BF16)
    slot_id = jnp.sum(jnp.where(inside, (column - first).astype(F32), 0.0), axis=0, keepdims=True)
    dims = (((0,), (0,)), ((), ()))
    for i, out in zip(places, outs):
        band = slice(i * rows, (i + 1) * rows)
        slot = lax.dot_general(
            slot_ref[:, band].astype(BF16), spread, dims, preferred_element_type=F32
        )
        weight = lax.dot_general(
            weight_ref[:, band].astype(BF16), spread, dims, preferred_element_type=F32
        )
        matrix = jnp.where(slot == slot_id, weight, 0.0).astype(BF16)
        term = jnp.dot(matrix, returned[...], preferred_element_type=F32)
        out[...] = term.astype(out.dtype)


def plane_exchange(rows):
    rows = rows.reshape(PLANE, SLOTS, -1)
    rows = lax.all_to_all(rows, ("y", "x"), split_axis=0, concat_axis=0, tiled=True)
    return rows.reshape(PLANE * SLOTS, -1)


def per_device(
    queries,
    key_rows,
    value_rows,
    hidden_in,
    out_proj,
    norm_gain,
    gate_up,
    down_proj,
    expert_ids,
    route_weight,
):
    tp_rank = lax.axis_index("tp")
    coords = jnp.stack([lax.axis_index(a) for a in ("y", "x", "z", "tp")]).astype(jnp.int32)
    rows, width = hidden_in.shape
    half = width // 2
    heads_in, columns = out_proj.shape
    inner = gate_up.shape[3]

    joined, packed = call(
        pack_kernel,
        (shaped((rows, queries.shape[1] + 2 * HD)), shaped((columns, 2 * heads_in + HD))), coords,
        out_proj.T, queries, key_rows, value_rows, expert_ids.T, route_weight.T,
        moved=1 << 20, mib=60, ins=[ANY] * 6,
        scratch=[
            pltpu.VMEM(expert_ids.T.shape, jnp.int32),
            pltpu.VMEM(route_weight.T.shape, F32),
            pltpu.SemaphoreType.DMA((6,)),
        ],
    )
    qkv = ring4(joined, "x")
    weight_z, anchor, meta = call(
        unpack_kernel,
        (shaped((NZ * columns, heads_in)), shaped((rows, 2 * HD)), shaped((NZ * 16, rows))),
        coords, *ring8(packed, "z"), moved=2 << 20, mib=8,
    )
    anchor = from_first(anchor)
    weight_y = ring4(weight_z, "y")
    table = shaped((PLANE, len(GROUPS[0]) * rows), F32)
    tables = call(routing_kernel, (table,) * 4, coords, meta, moved=1 << 18, mib=4)
    head_out = call(
        attend_kernel, shaped((NX * rows, heads_in)), coords, *qkv, anchor,
        flops=2 * 10**9, moved=6 << 20,
    )
    share = (NX * rows, width // (2 * NX))
    keep, give = call(
        project_kernel, (shaped(share, F32), shaped(share)), coords, head_out, *weight_y,
        scratch=[pltpu.VMEM((NY * rows, heads_in), BF16)], flops=10**9, moved=5 << 20,
    )
    other_half = swap(give)
    summed = [
        (keep[r * rows : (r + 1) * rows] + other_half[r * rows : (r + 1) * rows]).astype(BF16)
        for r in range(NX)
    ]
    pieces = summed[:1] + [shift(summed[r], "x", NX, r) for r in (1, 2, 3)]
    resid, sum_sq = call(
        residual_kernel, (shaped((rows, half)), shaped((rows, 1), F32)), coords, *pieces, hidden_in,
        ins=[ANY] * 5, moved=1 << 20, mib=4,
        scratch=[
            pltpu.VMEM((NX, rows, half // NX), BF16),
            pltpu.VMEM((rows, half), BF16),
            pltpu.SemaphoreType.DMA((5,)),
        ],
    )
    resid_float = resid.astype(F32)
    mean_sq = (sum_sq + swap(sum_sq)) / width
    gain_half = lax.dynamic_slice_in_dim(norm_gain, tp_rank * half, half, 0)
    normed = (resid_float * lax.rsqrt(mean_sq + 1e-06) * gain_half.astype(F32)).astype(BF16)

    gate_up = gate_up[0].reshape(width, 2 * inner)
    count = PLANE * SLOTS

    def dispatch(group, table, column, after=()):
        return call(
            pick_kernel, shaped((count, half)), coords, table, *[column[r] for r in group],
            ins=[VMEM] + [ANY] * len(group), outs=HBM, flops=7 * 10**8, moved=3 << 20, after=after,
            scratch=[
                pltpu.VMEM((len(group) * rows, half), BF16),
                pltpu.VMEM((count, len(group) * rows), BF16),
                pltpu.VMEM((count, half), BF16),
                pltpu.SemaphoreType.DMA((len(group),)),
            ],
        )

    def experts(own_part, other_part, after=()):
        return call(
            expert_kernel, (shaped((count, inner)), shaped((count, half))), coords,
            own_part, other_part, gate_up, down_proj[0],
            flops=5 * 10**9, moved=12 << 20, mib=14, after=after,
        )

    def finish(hidden, came, after=()):
        return call(
            down_kernel, shaped((count, half)), coords, hidden, down_proj[0], came,
            flops=10**9, moved=6 << 20, after=after,
        )

    terms = [None] * NZ

    def combine(group, wanted, slot, weight, returned, after=()):
        parts = call(
            functools.partial(combine_kernel, [group.index(r) for r in wanted]),
            tuple(shaped((rows, half), BF16 if r in (4, 5) else F32) for r in wanted),
            coords, slot, weight, returned, flops=7 * 10**8, moved=4 << 20, after=after,
        )
        for r, part in zip(wanted, parts):
            terms[r] = part

    first, second = GROUPS
    column = [None] * NZ
    column[0] = normed
    column[1], column[7] = shift(normed, "z", NZ, -1), shift(normed, "z", NZ, 1)
    column[2], column[6] = shift(column[1], "z", NZ, -1), shift(column[7], "z", NZ, 1)
    send_a = dispatch(first, tables[0], column, after=[gate_up])
    column[2], column[6], send_a = lax.optimization_barrier((column[2], column[6], send_a))
    column[3], column[5] = shift(column[2], "z", NZ, -1), shift(column[6], "z", NZ, 1)
    column[4] = shift(column[5], "z", NZ, 1)
    arrived_a = plane_exchange(send_a)
    send_b = dispatch(second, tables[2], column)
    send_b, arrived_a = lax.optimization_barrier((send_b, arrived_a))
    arrived_b = plane_exchange(send_b)
    hidden_a, other_a = experts(arrived_a, swap(arrived_a), after=[arrived_b])
    hidden_b, other_b = experts(arrived_b, swap(arrived_b), after=[hidden_a])
    done_a = finish(hidden_a, swap(other_a))
    returned_b = plane_exchange(finish(hidden_b, swap(other_b), after=[done_a]))
    returned_a = plane_exchange(done_a)
    combine(second, second, tables[2], tables[3], returned_b)
    went = terms[3] + shift(terms[4], "z", NZ, 1).astype(F32)
    came = terms[6] + shift(terms[5], "z", NZ, -1).astype(F32)
    went, came = shift(went.astype(BF16), "z", NZ, 1), shift(came.astype(BF16), "z", NZ, -1)
    combine(first, (2, 7), tables[0], tables[1], returned_a, after=[went, came])
    combine(first, (1, 0), tables[0], tables[1], returned_a, after=[terms[2]])
    went = shift((terms[2] + went.astype(F32)).astype(BF16), "z", NZ, 1)
    came = shift((terms[7] + came.astype(F32)).astype(BF16), "z", NZ, -1)
    went = shift((terms[1] + went.astype(F32)).astype(BF16), "z", NZ, 1)
    moe_sum = terms[0] + went.astype(F32) + came.astype(F32)
    return (resid_float + moe_sum).astype(BF16)


def solution(mesh):
    fine = Mesh(mesh.devices.reshape(NY, NX, NZ, 2), ("y", "x", "z", "tp"))
    ctx = ("y", "x", "z")
    in_specs = (
        P(ctx, "tp"),
        P(ctx, "tp"),
        P(ctx, "tp"),
        P(ctx, None),
        P("tp", ctx),
        P(),
        P(ctx, None, None, "tp"),
        P(ctx, "tp", None),
        P(ctx, None),
        P(ctx, None),
    )
    return jax.shard_map(
        per_device, mesh=fine, in_specs=in_specs, out_specs=P(ctx, "tp"), check_vma=False
    )
```

```python
import functools

import jax
import jax.numpy as jnp
from jax import lax
from jax.experimental import pallas as pl
from jax.experimental.pallas import tpu as pltpu
from jax.sharding import Mesh, PartitionSpec as P

HD = 128
NY, NX, NZ = 4, 4, 8
PLANE = NY * NX
CAP = 10
GROUPS = ((0, 1, 2, 7), (3, 4, 5, 6))
SLOTS = len(GROUPS[0]) * CAP
F32 = jnp.float32
BF16 = jnp.bfloat16
VMEM = pl.BlockSpec(memory_space=pltpu.VMEM)
SMEM = pl.BlockSpec(memory_space=pltpu.SMEM)
HBM = pl.BlockSpec(memory_space=pltpu.HBM)
ANY = pl.BlockSpec(memory_space=pl.ANY)


def shift(x, axis, size, step):
    return lax.ppermute(x, axis, [(i, (i + step) % size) for i in range(size)])


def swap(x):
    return lax.ppermute(x, "tp", [(0, 1), (1, 0)])


def call(
    kernel, out, coords, *arrays,
    scratch=(), flops=0, moved=0, mib=12, ins=None, outs=None, after=(),
):
    lead = [] if coords is None else [coords]

    def body(*refs):
        kernel(*(refs[:1] if lead else [None]), *refs[len(lead) + len(after) :])

    return pl.pallas_call(
        body,
        out_shape=out,
        in_specs=[SMEM] * len(lead) + [ANY] * len(after) + (ins or [VMEM] * len(arrays)),
        out_specs=outs or jax.tree.map(lambda _: VMEM, out),
        scratch_shapes=list(scratch),
        cost_estimate=pl.CostEstimate(flops=flops, bytes_accessed=moved, transcendentals=0),
        compiler_params=pltpu.CompilerParams(vmem_limit_bytes=mib * 1024 * 1024),
    )(*lead, *after, *arrays)


def shaped(shape, dtype=BF16):
    return jax.ShapeDtypeStruct(shape, dtype)


def from_first(x):
    for axis, size in (("x", NX), ("y", NY)):
        place = lax.axis_index(axis)
        have = 1
        while have < size:
            came = lax.ppermute(x, axis, [(k, k + have) for k in range(have)])
            x = jnp.where((place >= have) & (place < 2 * have), came, x)
            have *= 2
    return x


def ring8(x, axis):
    behind, ahead = [x], [x]
    for _ in range(3):
        behind.append(shift(behind[-1], axis, 8, 1))
        ahead.append(shift(ahead[-1], axis, 8, -1))
    return (*ahead, shift(behind[3], axis, 8, 1), behind[3], behind[2], behind[1])


def ring4(x, axis):
    behind, ahead = shift(x, axis, 4, 1), shift(x, axis, 4, -1)
    return x, ahead, shift(ahead, axis, 4, -1), behind


def fetch(pairs, sems):
    copies = [pltpu.make_async_copy(a, b, sems.at[i]) for i, (a, b) in enumerate(pairs)]
    for copy in copies:
        copy.start()
    for copy in copies:
        copy.wait()


def pack_kernel(
    coords, out_proj, queries, keys, values, ids_in, route_in, joined, out, ids, route, sems
):
    rows = out.shape[0]
    depth, wide = out_proj.shape[1], queries.shape[1]
    fetch(
        (
            (keys, joined.at[:, wide : wide + HD]),
            (values, joined.at[:, wide + HD :]),
            (out_proj, out.at[:, :depth]),
            (ids_in, ids),
            (route_in, route),
            (queries, joined.at[:, :wide]),
        ),
        sems,
    )
    for i in range(keys.shape[0] // rows):
        at = depth + i * 2 * HD
        out[:, at : at + 2 * HD] = joined[i * rows : (i + 1) * rows, wide:]
    mix = route[...] / jnp.sum(route[...], axis=0, keepdims=True)
    meta = jnp.concatenate([ids[...].astype(F32), mix], axis=0)
    out[:, out.shape[1] - HD :] = meta.astype(BF16)


def unpack_kernel(coords, *refs):
    *blocks, weight, first, meta, own, sems = refs
    z = coords[2]
    fetch([(blocks[0], own)], sems)
    blocks[0] = own
    rows = blocks[0].shape[0]
    depth = weight.shape[1]
    for r, ref in enumerate(blocks):
        owner = lax.rem(z + r, NZ)
        weight[pl.ds(pl.multiple_of(owner * rows, rows), rows), :] = ref[:, :depth]
        meta[r * rows : (r + 1) * rows, :] = ref[:, ref.shape[1] - HD :]

        @pl.when(owner == 0)
        def _(ref=ref):
            for i in range(first.shape[0] // rows):
                at = depth + i * 2 * HD
                first[i * rows : (i + 1) * rows, :] = ref[:, at : at + 2 * HD]


def attend_kernel(coords, own, ahead, far, behind, anchor, head_out):
    y, x, z = coords[0], coords[1], coords[2]
    rows = own.shape[0]
    wide = own.shape[1] - 2 * HD
    batch = 4
    shape = (batch * rows, 2 * rows)
    row_id = lax.rem(lax.broadcasted_iota(jnp.int32, shape, 0), rows)
    col_id = lax.broadcasted_iota(jnp.int32, shape, 1)
    own_ok = (col_id >= rows) & (col_id - rows <= row_id)
    for r, qkv in enumerate((own, ahead, far, behind)):
        live = (y + lax.rem(x + r, NX) + z) > 0
        visible = own_ok | ((col_id < rows) & live)
        band = slice(r * rows, (r + 1) * rows)
        keys = jnp.concatenate([anchor[:, :HD], qkv[:, wide : wide + HD]], axis=0)
        values = jnp.concatenate([anchor[:, HD:], qkv[:, wide + HD :]], axis=0)
        for first in range(0, wide // HD, batch):
            heads = range(first, first + batch)
            query = jnp.concatenate([qkv[:, h * HD : (h + 1) * HD] for h in heads], axis=0)
            scores = lax.dot_general(
                query, keys, (((1,), (1,)), ((), ())), preferred_element_type=F32
            ) * HD ** (-0.5)
            scores = jnp.where(visible, scores, -1e30)
            exp_scores = jnp.exp(scores - jnp.max(scores, axis=-1, keepdims=True))
            probs = exp_scores * (1.0 / jnp.sum(exp_scores, axis=-1, keepdims=True))
            result = jnp.dot(probs.astype(BF16), values, preferred_element_type=F32).astype(BF16)
            for i, h in enumerate(heads):
                head_out[band, h * HD : (h + 1) * HD] = result[i * rows : (i + 1) * rows]


def project_kernel(coords, head_out, own, ahead, far, behind, keep_ref, give_ref, weight):
    y, t = coords[0], coords[3]
    rows = own.shape[0]
    for r, ref in enumerate((own, ahead, far, behind)):
        at = lax.rem(y + r + NY - 2 * t, NY) * rows
        weight[pl.ds(pl.multiple_of(at, rows), rows), :] = ref[...]
    cut = keep_ref.shape[1]
    dims = (((1,), (1,)), ((), ()))
    for ref, part in ((give_ref, slice(cut, 2 * cut)), (keep_ref, slice(0, cut))):
        result = lax.dot_general(
            head_out[...], weight[part, :], dims, preferred_element_type=F32
        )
        ref[...] = result.astype(ref.dtype)


def residual_kernel(
    coords, p0, p1, p2, p3, hidden, resid_ref, sq_ref, pieces, hidden_buf, sems
):
    x, t = coords[1], coords[3]
    rows, half = resid_ref.shape
    hidden_half = hidden.at[:, pl.ds(pl.multiple_of(t * half, half), half)]
    fetch(
        [(p, pieces.at[r]) for r, p in enumerate((p0, p1, p2, p3))] + [(hidden_half, hidden_buf)],
        sems,
    )
    total = jnp.zeros((rows, 1), F32)
    for r in range(NX):
        for part in range(2):
            at = (part * NX + lax.rem(x + NX - r, NX)) * HD
            at = pl.ds(pl.multiple_of(at, HD), HD)
            term = pieces[r, :, part * HD : (part + 1) * HD].astype(F32)
            resid = (hidden_buf[:, at].astype(F32) + term).astype(BF16)
            resid_ref[:, at] = resid
            total += jnp.sum(jnp.square(resid.astype(F32)), axis=-1, keepdims=True)
    sq_ref[...] = total


def routing_kernel(coords, meta, *tables):
    z = coords[2]
    rows = meta.shape[1]
    top = meta.shape[0] // (2 * NZ)
    gathered = meta[...].astype(F32)
    before = lax.broadcasted_iota(jnp.int32, (rows, rows), 0) < lax.broadcasted_iota(
        jnp.int32, (rows, rows), 1
    )
    before = before.astype(F32).astype(BF16)
    expert = lax.broadcasted_iota(jnp.int32, (PLANE, top, rows), 0) * NZ + z
    for g, group in enumerate(GROUPS):
        for i, r in enumerate(group):
            table = gathered[2 * r * top : 2 * (r + 1) * top, :]
            hit = table[None, :top].astype(jnp.int32) == expert
            named = jnp.sum(jnp.where(hit, 1.0, 0.0), axis=1)
            weight = jnp.sum(jnp.where(hit, table[None, top:], 0.0), axis=1)
            slot = jnp.dot(named.astype(BF16), before, preferred_element_type=F32)
            slot = jnp.where(named > 0.5, slot + float(i * CAP), -1.0)
            tables[2 * g][:, i * rows : (i + 1) * rows] = slot
            tables[2 * g + 1][:, i * rows : (i + 1) * rows] = weight


def pick_kernel(coords, slot_ref, *refs):
    *blocks, out, column, pick, result, sems = refs
    rows = blocks[0].shape[0]
    fetch([(b, column.at[i * rows : (i + 1) * rows, :]) for i, b in enumerate(blocks)], sems)
    slot_id = lax.broadcasted_iota(jnp.int32, (SLOTS, column.shape[0]), 0).astype(F32)
    for p in range(PLANE):
        hit = slot_ref[p : p + 1, :] == slot_id
        pick[p * SLOTS : (p + 1) * SLOTS, :] = jnp.where(hit, 1.0, 0.0).astype(BF16)
    for q in range(2):
        band = slice(q * 320, (q + 1) * 320)
        result[band, :] = jnp.dot(
            pick[band, :], column[...], preferred_element_type=F32
        ).astype(BF16)
    fetch([(result, out)], sems)


def expert_kernel(coords, own, other, gate_up, down, hidden, out):
    t = coords[3]
    depth = own.shape[1]
    inner = hidden.shape[1]
    mine = pl.ds(pl.multiple_of(t * depth, depth), depth)
    theirs = pl.ds(pl.multiple_of((1 - t) * depth, depth), depth)
    tile = 256
    for c in range(0, inner, tile):
        gate, up = (
            jnp.dot(own[...], gate_up[mine, at : at + tile], preferred_element_type=F32)
            + jnp.dot(other[...], gate_up[theirs, at : at + tile], preferred_element_type=F32)
            for at in (c, inner + c)
        )
        hidden[:, c : c + tile] = (gate / (1.0 + jnp.exp(-gate)) * up).astype(BF16)
    out[...] = jnp.dot(hidden[...], down[:, theirs], preferred_element_type=F32).astype(BF16)


def down_kernel(coords, hidden, down, came, out):
    depth = came.shape[1]
    mine = pl.ds(pl.multiple_of(coords[3] * depth, depth), depth)
    total = jnp.dot(hidden[...], down[:, mine], preferred_element_type=F32)
    out[...] = (total + came[...].astype(F32)).astype(BF16)


def combine_kernel(places, coords, slot_ref, weight_ref, returned, *outs):
    rows = outs[0].shape[0]
    total = PLANE * SLOTS
    column = lax.broadcasted_iota(jnp.int32, (PLANE, total), 1)
    first = lax.broadcasted_iota(jnp.int32, (PLANE, total), 0) * SLOTS
    inside = (column >= first) & (column < first + SLOTS)
    spread = jnp.where(inside, 1.0, 0.0).astype(BF16)
    slot_id = jnp.sum(jnp.where(inside, (column - first).astype(F32), 0.0), axis=0, keepdims=True)
    dims = (((0,), (0,)), ((), ()))
    for i, out in zip(places, outs):
        band = slice(i * rows, (i + 1) * rows)
        slot = lax.dot_general(
            slot_ref[:, band].astype(BF16), spread, dims, preferred_element_type=F32
        )
        weight = lax.dot_general(
            weight_ref[:, band].astype(BF16), spread, dims, preferred_element_type=F32
        )
        matrix = jnp.where(slot == slot_id, weight, 0.0).astype(BF16)
        term = jnp.dot(matrix, returned[...], preferred_element_type=F32)
        out[...] = term.astype(out.dtype)


def plane_exchange(rows):
    rows = rows.reshape(PLANE, SLOTS, -1)
    rows = lax.all_to_all(rows, ("y", "x"), split_axis=0, concat_axis=0, tiled=True)
    return rows.reshape(PLANE * SLOTS, -1)


def per_device(
    queries,
    key_rows,
    value_rows,
    hidden_in,
    out_proj,
    norm_gain,
    gate_up,
    down_proj,
    expert_ids,
    route_weight,
):
    tp_rank = lax.axis_index("tp")
    coords = jnp.stack([lax.axis_index(a) for a in ("y", "x", "z", "tp")]).astype(jnp.int32)
    rows, width = hidden_in.shape
    half = width // 2
    heads_in, columns = out_proj.shape
    inner = gate_up.shape[3]

    joined, packed = call(
        pack_kernel,
        (shaped((rows, queries.shape[1] + 2 * HD)), shaped((columns, 2 * heads_in + HD))), None,
        out_proj.T, queries, key_rows, value_rows, expert_ids.T, route_weight.T,
        moved=1 << 20, mib=60, ins=[ANY] * 6,
        scratch=[
            pltpu.VMEM(expert_ids.T.shape, jnp.int32),
            pltpu.VMEM(route_weight.T.shape, F32),
            pltpu.SemaphoreType.DMA((6,)),
        ],
    )
    qkv = ring4(joined, "x")
    weight_z, anchor, meta = call(
        unpack_kernel,
        (shaped((NZ * columns, heads_in)), shaped((rows, 2 * HD)), shaped((NZ * 16, rows))),
        coords, *ring8(packed, "z"), moved=2 << 20, mib=8, ins=[ANY] + [VMEM] * 7,
        scratch=[pltpu.VMEM(packed.shape, BF16), pltpu.SemaphoreType.DMA((1,))],
    )
    anchor = from_first(anchor)
    weight_y = ring4(weight_z, "y")
    table = shaped((PLANE, len(GROUPS[0]) * rows), F32)
    tables = call(routing_kernel, (table,) * 4, coords, meta, moved=1 << 18, mib=4)
    head_out = call(
        attend_kernel, shaped((NX * rows, heads_in)), coords, *qkv, anchor,
        flops=2 * 10**9, moved=6 << 20,
    )
    share = (NX * rows, width // (2 * NX))
    keep, give = call(
        project_kernel, (shaped(share, F32), shaped(share)), coords, head_out, *weight_y,
        scratch=[pltpu.VMEM((NY * rows, heads_in), BF16)], flops=10**9, moved=5 << 20,
    )
    other_half = swap(give)
    summed = [
        (keep[r * rows : (r + 1) * rows] + other_half[r * rows : (r + 1) * rows]).astype(BF16)
        for r in range(NX)
    ]
    pieces = summed[:1] + [shift(summed[r], "x", NX, r) for r in (1, 2, 3)]
    resid, sum_sq = call(
        residual_kernel, (shaped((rows, half)), shaped((rows, 1), F32)), coords, *pieces, hidden_in,
        ins=[ANY] * 5, moved=1 << 20, mib=4,
        scratch=[
            pltpu.VMEM((NX, rows, half // NX), BF16),
            pltpu.VMEM((rows, half), BF16),
            pltpu.SemaphoreType.DMA((5,)),
        ],
    )
    resid_float = resid.astype(F32)
    mean_sq = (sum_sq + swap(sum_sq)) / width
    gain_half = lax.dynamic_slice_in_dim(norm_gain, tp_rank * half, half, 0)
    normed = (resid_float * lax.rsqrt(mean_sq + 1e-06) * gain_half.astype(F32)).astype(BF16)

    gate_up = gate_up[0].reshape(width, 2 * inner)
    count = PLANE * SLOTS

    def dispatch(group, table, column, after=()):
        return call(
            pick_kernel, shaped((count, half)), coords, table, *[column[r] for r in group],
            ins=[VMEM] + [ANY] * len(group), outs=HBM, flops=7 * 10**8, moved=3 << 20, after=after,
            scratch=[
                pltpu.VMEM((len(group) * rows, half), BF16),
                pltpu.VMEM((count, len(group) * rows), BF16),
                pltpu.VMEM((count, half), BF16),
                pltpu.SemaphoreType.DMA((len(group),)),
            ],
        )

    def experts(own_part, other_part, after=()):
        return call(
            expert_kernel, (shaped((count, inner)), shaped((count, half))), coords,
            own_part, other_part, gate_up, down_proj[0],
            flops=5 * 10**9, moved=12 << 20, mib=14, after=after,
        )

    def finish(hidden, came, after=()):
        return call(
            down_kernel, shaped((count, half)), coords, hidden, down_proj[0], came,
            flops=10**9, moved=6 << 20, after=after,
        )

    terms = [None] * NZ

    def combine(group, wanted, slot, weight, returned, after=()):
        parts = call(
            functools.partial(combine_kernel, [group.index(r) for r in wanted]),
            tuple(shaped((rows, half), BF16 if r in (4, 5) else F32) for r in wanted),
            coords, slot, weight, returned, flops=7 * 10**8, moved=4 << 20, after=after,
        )
        for r, part in zip(wanted, parts):
            terms[r] = part

    first, second = GROUPS
    column = [None] * NZ
    column[0] = normed
    column[1], column[7] = shift(normed, "z", NZ, -1), shift(normed, "z", NZ, 1)
    column[2], column[6] = shift(column[1], "z", NZ, -1), shift(column[7], "z", NZ, 1)
    send_a = dispatch(first, tables[0], column, after=[gate_up])
    column[2], column[6], send_a = lax.optimization_barrier((column[2], column[6], send_a))
    column[3], column[5] = shift(column[2], "z", NZ, -1), shift(column[6], "z", NZ, 1)
    column[4] = shift(column[5], "z", NZ, 1)
    arrived_a = plane_exchange(send_a)
    send_b = dispatch(second, tables[2], column)
    send_b, arrived_a = lax.optimization_barrier((send_b, arrived_a))
    arrived_b = plane_exchange(send_b)
    hidden_a, other_a = experts(arrived_a, swap(arrived_a), after=[arrived_b])
    hidden_b, other_b = experts(arrived_b, swap(arrived_b), after=[hidden_a])
    done_a = finish(hidden_a, swap(other_a))
    returned_b = plane_exchange(finish(hidden_b, swap(other_b), after=[done_a]))
    returned_a = plane_exchange(done_a)
    combine(second, second, tables[2], tables[3], returned_b)
    went = terms[3] + shift(terms[4], "z", NZ, 1).astype(F32)
    came = terms[6] + shift(terms[5], "z", NZ, -1).astype(F32)
    went, came = shift(went.astype(BF16), "z", NZ, 1), shift(came.astype(BF16), "z", NZ, -1)
    combine(first, (2, 7), tables[0], tables[1], returned_a, after=[went, came])
    combine(first, (1, 0), tables[0], tables[1], returned_a, after=[terms[2]])
    went = shift((terms[2] + went.astype(F32)).astype(BF16), "z", NZ, 1)
    came = shift((terms[7] + came.astype(F32)).astype(BF16), "z", NZ, -1)
    went = shift((terms[1] + went.astype(F32)).astype(BF16), "z", NZ, 1)
    moe_sum = terms[0] + went.astype(F32) + came.astype(F32)
    return (resid_float + moe_sum).astype(BF16)


def solution(mesh):
    fine = Mesh(mesh.devices.reshape(NY, NX, NZ, 2), ("y", "x", "z", "tp"))
    ctx = ("y", "x", "z")
    in_specs = (
        P(ctx, "tp"),
        P(ctx, "tp"),
        P(ctx, "tp"),
        P(ctx, None),
        P("tp", ctx),
        P(),
        P(ctx, None, None, "tp"),
        P(ctx, "tp", None),
        P(ctx, None),
        P(ctx, None),
    )
    return jax.shard_map(
        per_device, mesh=fine, in_specs=in_specs, out_specs=P(ctx, "tp"), check_vma=False
    )
```
